256 devices in a mesh: wave: 128 (over z, x, y), deg: 2 (over core).
Axes of the slice: x: 4, y: 4, z: 8, core: 2. Of those that a mesh axis runs over, the one named last changes fastest.
Arguments:
- wind_u: bfloat16 [16, 2, 1280, 5120], P('deg', None, 'wave'), may hold values from -6 to 6
- wind_v: bfloat16 [16, 2, 1280, 5120], P('deg', None, 'wave'), may hold values from -6 to 6
- window_m: int32 [256], replicated, may hold values from 1280 to 2559, as said below
- owner: int32 [256], replicated, may hold values from 0 to 127, as said below
- legendre: bfloat16 [512, 1280, 1280], P('wave', None, 'deg'), may hold values from -12 to 12
Outputs:
- coeffs: float32 [512, 2, 16, 2, 1280], P('wave', None, None, None, 'deg')
- spectra: float32 [2, 16, 1280], P(None, None, ('wave', 'deg'))
The draws below stay inside these ranges and needn't reach their ends.
Inputs may be any that keep to these rules, and one draw needn't show every extreme that they name: `window_m`: the window's entries name distinct wavenumbers. `owner`: no index appears in more than 4 entries, and some index appears in exactly 4.
All inputs are finite; a program needn't handle non-finite values.
Results may differ from the reference program's by a relative error of at most 0.01.
Values may be sent and summed in bfloat16 or wider, within the bound.
A program may use at most 128 MiB of HBM per device.

```python
import jax
import jax.numpy as jnp
from jax import lax

NLON = 5120
NHALF = 1280
CAP = 4
KDEG = 1280
NMAX = 2559
LEV = 16
MW = 256
SLOTS = 512


def draw_window_m(key, part):
    key = jax.random.fold_in(key, 11)
    picked = jax.random.permutation(key, KDEG)[:MW]
    return (picked + NHALF).astype(jnp.int32)


def draw_owner(key, part):
    key = jax.random.fold_in(key, 23)
    key_dev, key_rank, key_order = jax.random.split(key, 3)
    devices = SLOTS // CAP
    chosen_dev = jax.random.randint(key_dev, (), 0, devices)
    scores = jax.random.permutation(key_rank, SLOTS).astype(jnp.int32)
    slot_ids = jnp.arange(SLOTS, dtype=jnp.int32)
    scores = scores + SLOTS * (slot_ids // CAP == chosen_dev).astype(jnp.int32)
    top_scores, picked = lax.top_k(scores, MW)
    shuffle = jax.random.permutation(key_order, MW)
    return (picked[shuffle] // CAP).astype(jnp.int32)


def steps_of(rng, shape, cuts, low, largest):
    def one(axis_at, shards_of):
        heights = jax.random.uniform(jax.random.fold_in(jax.random.fold_in(rng, 6), axis_at), (shards_of,), jnp.float32, low / len(cuts), largest / len(cuts))
        return jnp.repeat(jnp.exp(heights), shape[axis_at] // shards_of).reshape((-1,) + (1,) * (len(shape) - axis_at - 1))

    factor_of = one(*cuts[0])
    for cut in cuts[1:]:
        factor_of = factor_of * one(*cut)
    return factor_of


def bell_draw(own_key, shape, deviation, most, shards=(), held_as=jnp.bfloat16):
    result = deviation * jax.random.normal(own_key, shape, jnp.float32)
    if shards:
        result = result * steps_of(own_key, shape, shards, -0.22, 0.18)
    return jnp.clip(result, -most, most).astype(held_as)


def setup_inputs(seed: int = 0) -> dict:
    keys = jax.random.split(jax.random.key(seed), 6)
    wind_u = bell_draw(keys[0], (LEV, 2, NHALF, NLON), 1.0, 6.0, ((0, 2), (2, 128)))
    wind_v = bell_draw(keys[1], (LEV, 2, NHALF, NLON), 1.0, 6.0, ((0, 2), (2, 128)))
    window_m = draw_window_m(jax.random.fold_in(keys[5], 71), 0)
    owner = draw_owner(jax.random.fold_in(keys[5], 71), 0)
    legendre = bell_draw(keys[4], (SLOTS, NHALF, KDEG), 2.0, 12.0, ((0, 128), (2, 2)))
    return {"wind_u": wind_u, "wind_v": wind_v, "window_m": window_m, "owner": owner, "legendre": legendre}


def slot_numbers(owner):
    positions = jnp.arange(owner.shape[0], dtype=jnp.int32)
    same_owner = (owner[:, None] == owner[None, :]) & (positions[None, :] < positions[:, None])
    return owner * CAP + lax.optimization_barrier(jnp.sum(same_owner.astype(jnp.int32), axis=1))

def times_unit(values):
    return jnp.stack([-values[..., 1, :], values[..., 0, :]], axis=-2)

def spectral_terms(flow_u, flow_v, wave_int, degree_int):
    wave_num = wave_int.astype(jnp.float32)
    degree = degree_int.astype(jnp.float32)
    next_degree = degree_int + 1
    eps_here = jnp.sqrt((degree_int * degree_int - wave_int * wave_int).astype(jnp.float32) / (4.0 * degree * degree - 1.0))
    eps_next = jnp.sqrt((next_degree * next_degree - wave_int * wave_int).astype(jnp.float32) / (4.0 * (degree + 1.0) * (degree + 1.0) - 1.0))
    low_term = (degree + 1.0) * eps_here
    high_term = degree * eps_next
    centre_u = flow_u[..., 1:-1]
    centre_v = flow_v[..., 1:-1]
    vorticity = wave_num * times_unit(centre_v) + low_term * flow_u[..., :-2] - high_term * flow_u[..., 2:]
    divergence = wave_num * times_unit(centre_u) - low_term * flow_v[..., :-2] + high_term * flow_v[..., 2:]
    return jnp.stack([vorticity, divergence], axis=-4) * lax.rsqrt(degree * (degree + 1.0))

def reference(wind_u, wind_v, window_m, owner, legendre):

    def per_level(level_index):
        level_winds = jnp.stack([wind_u[level_index], wind_v[level_index]]).astype(jnp.float32)
        spectrum_rows = jnp.fft.rfft(level_winds, axis=-1)[..., window_m] / NLON
        return jnp.stack([jnp.real(spectrum_rows), jnp.imag(spectrum_rows)], axis=2)
    fourier = lax.map(per_level, jnp.arange(LEV, dtype=jnp.int32))
    paired = jnp.stack([fourier[:, :, 0] + fourier[:, :, 1], fourier[:, :, 0] - fourier[:, :, 1]]).astype(jnp.bfloat16)
    slot_of = slot_numbers(owner)
    degrees = jnp.arange(KDEG, dtype=jnp.int32)

    def one_entry(entry_index):
        legendre_rows = legendre[slot_of[entry_index]].astype(jnp.float32)
        entry_data = paired[..., entry_index].astype(jnp.float32)
        both_par = jnp.einsum('plfcj,jk->plfck', entry_data, legendre_rows)
        projection = jnp.where(degrees % 2 == 0, both_par[0], both_par[1])
        wave_int = window_m[entry_index]
        degree_int = wave_int + degrees
        live_cols = degree_int <= NMAX
        projection = jnp.where(live_cols, projection, 0.0)
        empty_col = jnp.zeros(projection.shape[:-1] + (1,), projection.dtype)
        padded_ext = jnp.concatenate([empty_col, projection, empty_col], axis=-1)
        entry_coeffs = spectral_terms(padded_ext[:, 0], padded_ext[:, 1], wave_int, degree_int)
        entry_coeffs = jnp.where(live_cols, entry_coeffs, 0.0)
        energy = lax.optimization_barrier(jnp.sum(entry_coeffs * entry_coeffs, axis=2))
        buffer = jnp.zeros((2, LEV, 2 * KDEG), jnp.float32)
        start_index = (wave_int - NHALF).astype(jnp.int32)
        placed = lax.dynamic_update_slice(buffer, energy, (jnp.int32(0), jnp.int32(0), start_index))
        return (entry_coeffs, placed[:, :, :KDEG])
    all_coeffs, all_placed = lax.map(one_entry, jnp.arange(MW, dtype=jnp.int32))
    slot_coeffs = jnp.zeros((SLOTS, 2, LEV, 2, KDEG), jnp.float32).at[slot_of].set(all_coeffs)
    spectra = lax.optimization_barrier(jnp.sum(all_placed, axis=0)) / MW
    return (slot_coeffs, spectra)
```

```python
import functools
import math

import jax
import jax.numpy as jnp
import numpy as np
from jax import lax
from jax.experimental import pallas as pl
from jax.experimental.pallas import tpu as pltpu
from jax.sharding import PartitionSpec as P

MESH = pl.DeviceIdType.MESH
BF16 = jnp.bfloat16
F32 = jnp.float32
VMEM_BYTES = 56 * 1024 * 1024

NLON = 5120
LANES = 128
COARSE = NLON // LANES
ENTRIES = 256
ROWS = 10
HALF = 1280
COLS = 640
CHUNK = 4

NT = (((1,), (1,)), ((), ()))


def row_order():
    source = np.arange(640).reshape(2, 2, 2, 8, ROWS)
    wanted = source.transpose(4, 1, 2, 3, 0).reshape(-1)
    return np.eye(640, dtype=np.float32)[wanted].astype(jnp.bfloat16)


def group_order():
    source = np.arange(160).reshape(ROWS, 16)
    wanted = source.transpose(1, 0).reshape(-1)
    return np.eye(160, dtype=np.float32)[wanted].astype(jnp.bfloat16)


def unit_waves(steps, window, period):
    phase = steps * window
    phase = phase - period * jnp.round(phase * (1.0 / period))
    angle = phase * (2.0 * math.pi / period)
    return jnp.cos(angle), jnp.sin(angle)


def dft_kernel(
    wind_u, wind_v, window_ref, slot_ref, order_ref, group_ref, out_ref,
    winds, coarse_cos, coarse_sin, fine_cos, fine_sin, total, split, sems,
):
    for chunk in range(COARSE // CHUNK):
        for inner in range(CHUNK):
            tile = chunk * CHUNK + inner
            for which, ref in enumerate((wind_u, wind_v)):
                pltpu.make_async_copy(ref.at[:, tile], winds.at[tile, which], sems.at[chunk]).start()
    window = window_ref[...].astype(F32)
    coarse_steps = lax.broadcasted_iota(jnp.int32, (COARSE, ENTRIES), 0).astype(F32)
    fine_steps = lax.broadcasted_iota(jnp.int32, (LANES, ENTRIES), 0).astype(F32)
    cos_part, sin_part = unit_waves(coarse_steps, window, float(COARSE))
    coarse_cos[...] = cos_part
    coarse_sin[...] = sin_part
    cos_part, sin_part = unit_waves(fine_steps, window, float(NLON))
    fine_cos[...] = cos_part * (1.0 / NLON)
    fine_sin[...] = sin_part * (1.0 / NLON)
    total[...] = jnp.zeros_like(total)

    def step(chunk, carry):
        part = winds.at[pl.ds(chunk * CHUNK, CHUNK)]
        pltpu.make_async_copy(part, part, sems.at[chunk]).wait()
        cos_b = fine_cos[...]
        sin_b = fine_sin[...]
        highs, lows, pieces = [], [], []
        for inner in range(CHUNK):
            tile = chunk * CHUNK + inner
            cos_a = coarse_cos[pl.ds(tile, 1), :]
            sin_a = coarse_sin[pl.ds(tile, 1), :]
            table = jnp.concatenate(
                [cos_a * cos_b - sin_a * sin_b, -(sin_a * cos_b + cos_a * sin_b)], axis=1
            )
            high = table.astype(BF16)
            highs.append(high)
            lows.append((table - high.astype(F32)).astype(BF16))
            pieces.append(winds.at[tile].reshape(320, LANES)[...])
        data = jnp.concatenate(pieces, axis=1)
        total[...] += jnp.dot(
            data, jnp.concatenate(highs, axis=0), preferred_element_type=F32
        ) + jnp.dot(data, jnp.concatenate(lows, axis=0), preferred_element_type=F32)
        return carry

    lax.fori_loop(0, COARSE // CHUNK, step, 0)
    for tile in range(4):
        split[tile] = total[:, LANES * tile : LANES * tile + LANES]

    def hemisphere(h):
        return jnp.concatenate([split[tile, pl.ds(h, 160, stride=2), :] for tile in range(4)], axis=1)

    north = hemisphere(0)
    south = hemisphere(1)
    even = (north + south).astype(BF16)
    odd = (north - south).astype(BF16)
    paired = jnp.concatenate(
        [even[:, :ENTRIES], odd[:, :ENTRIES], even[:, ENTRIES:], odd[:, ENTRIES:]], axis=0
    )
    ordered = jnp.dot(order_ref[...], paired, preferred_element_type=F32).astype(BF16)
    empty = jnp.zeros((64, ENTRIES), BF16)
    blocks = []
    for row in range(ROWS):
        block = ordered[64 * row : 64 * row + 64]
        blocks.append(jnp.concatenate([block, empty], axis=1))
        blocks.append(jnp.concatenate([empty, block], axis=1))
    blocks = jnp.concatenate(blocks, axis=0)
    pair_ids = 2 * lax.broadcasted_iota(jnp.int32, (256, ENTRIES), 0)
    slots = slot_ref[...]
    placing = jnp.concatenate(
        [
            (slots == pair_ids).astype(F32).astype(BF16),
            (slots == pair_ids + 1).astype(F32).astype(BF16),
        ],
        axis=1,
    )
    placed = lax.dot_general(placing, blocks, NT, preferred_element_type=F32).astype(BF16)
    stacked = jnp.concatenate(
        [
            jnp.concatenate(
                [placed[16 * g : 16 * g + 16, LANES * row : LANES * row + LANES] for g in range(16)],
                axis=1,
            )
            for row in range(ROWS)
        ],
        axis=0,
    )
    result = jnp.dot(group_ref[...], stacked, preferred_element_type=F32).astype(BF16)
    for g in range(16):
        out_ref[160 * g : 160 * g + 160, :] = result[:, LANES * g : LANES * g + LANES]


def dft_call(wind_u, wind_v, window_m, slot_of):
    vmem = pl.BlockSpec(memory_space=pltpu.VMEM)
    hbm = pl.BlockSpec(memory_space=pl.ANY)

    def tiles(wind):
        split = wind.transpose(0, 2, 1, 3).reshape(8, ROWS, 2, COARSE, LANES)
        return split.transpose(0, 1, 3, 2, 4).reshape(80, COARSE, 2, LANES)

    return pl.pallas_call(
        dft_kernel,
        out_shape=jax.ShapeDtypeStruct((2560, LANES), BF16),
        in_specs=[hbm, hbm, vmem, vmem, vmem, vmem],
        out_specs=vmem,
        scratch_shapes=[
            pltpu.VMEM((COARSE, 2, 80, 2, LANES), BF16),
            pltpu.VMEM((COARSE, ENTRIES), F32),
            pltpu.VMEM((COARSE, ENTRIES), F32),
            pltpu.VMEM((LANES, ENTRIES), F32),
            pltpu.VMEM((LANES, ENTRIES), F32),
            pltpu.VMEM((320, 2 * ENTRIES), F32),
            pltpu.VMEM((4, 320, LANES), F32),
            pltpu.SemaphoreType.DMA((COARSE // CHUNK,)),
        ],
        compiler_params=pltpu.CompilerParams(vmem_limit_bytes=VMEM_BYTES),
    )(
        tiles(wind_u), tiles(wind_v), window_m[None, :], slot_of[None, :],
        jnp.asarray(row_order()), jnp.asarray(group_order()),
    )


def exchange_kernel(
    send_ref, table_ref, data_ref, edge_ref,
    send_sem, recv_sem, core_send, core_recv, edge_send, edge_recv,
):
    me = lax.axis_index("wave")
    core = lax.axis_index("deg")
    other = 1 - core
    plane = me // 16
    inside = me % 16

    def partner(step):
        return (plane + step // 16) % 8 * 16 + (inside // 4 + step // 4) % 4 * 4 + (inside + step) % 4

    barrier = pltpu.get_barrier_semaphore()

    def greet(step, carry):
        pl.semaphore_signal(barrier, inc=1, device_id=(partner(step), core), device_id_type=MESH)
        return carry

    lax.fori_loop(1, 128, greet, 0)
    pl.semaphore_signal(barrier, inc=1, device_id=(me, other), device_id_type=MESH)
    pl.semaphore_wait(barrier, 128)

    edge = pltpu.make_async_remote_copy(
        src_ref=table_ref.at[:, :, pl.ds(pl.multiple_of(other * 512, LANES), LANES)],
        dst_ref=edge_ref, send_sem=edge_send, recv_sem=edge_recv,
        device_id=(me, other), device_id_type=MESH,
    )
    own = pltpu.make_async_copy(send_ref.at[me], data_ref.at[core, :, me], recv_sem.at[0])
    own.start()

    def send(step, carry):
        target = partner(step)
        pltpu.make_async_remote_copy(
            src_ref=send_ref.at[target], dst_ref=data_ref.at[core, :, me],
            send_sem=send_sem, recv_sem=recv_sem.at[step // 16],
            device_id=(target, core), device_id_type=MESH,
        ).start()
        return carry

    lax.fori_loop(1, 128, send, 0)
    edge.start()

    def forward(step):
        group = (plane + 8 - step) % 8
        part = data_ref.at[core, :, pl.ds(group * 16, 16)]
        return part, pltpu.make_async_remote_copy(
            src_ref=part, dst_ref=part, send_sem=core_send.at[step], recv_sem=core_recv.at[step],
            device_id=(me, other), device_id_type=MESH,
        )

    for step in range(8):
        part, copy = forward(step)
        pltpu.make_async_copy(part, part, recv_sem.at[step]).wait()
        copy.start()
    for step in range(8):
        part, copy = forward(step)
        copy.wait_send()
        group = (plane + 8 - step) % 8
        arrived = data_ref.at[other, :, pl.ds(group * 16, 16)]
        pltpu.make_async_copy(arrived, arrived, core_recv.at[step]).wait()
    edge.wait()
    sent = send_ref.at[pl.ds(0, 127)]
    pltpu.make_async_copy(sent, sent, send_sem).wait()


def exchange_call(outgoing, legendre):
    hbm = pl.BlockSpec(memory_space=pl.ANY)
    dma = pltpu.SemaphoreType.DMA
    return pl.pallas_call(
        exchange_kernel,
        out_shape=(
            jax.ShapeDtypeStruct((2, 2, 128, 5, 2, LANES), BF16),
            jax.ShapeDtypeStruct((4, HALF, LANES), BF16),
        ),
        in_specs=[hbm, hbm],
        out_specs=(hbm, hbm),
        scratch_shapes=[dma, dma((8,)), dma((8,)), dma((8,)), dma, dma],
        compiler_params=pltpu.CompilerParams(
            collective_id=0, has_side_effects=True, vmem_limit_bytes=VMEM_BYTES
        ),
    )(outgoing.reshape(128, 2, 5, 2, LANES), legendre)


def project_kernel(meta, data_ref, table_ref, edge_ref, out_ref, energy_ref, summed, split):
    slot = pl.program_id(0)
    core = meta[8]
    wave_int = meta[slot]
    used = meta[4 + slot]
    half = slot % 2
    row_ids = lax.broadcasted_iota(jnp.int32, (64, LANES), 0)
    col_ids = lax.broadcasted_iota(jnp.int32, (64, LANES), 1)
    picking = (col_ids == row_ids + 64 * half).astype(F32).astype(BF16)
    rows = jnp.concatenate(
        [
            lax.dot_general(picking, data_ref[h, 0], NT, preferred_element_type=F32).astype(BF16)
            for h in range(2)
        ],
        axis=0,
    )
    main = jnp.dot(rows, table_ref[0], preferred_element_type=F32)
    beside = jnp.dot(rows, edge_ref[0], preferred_element_type=F32)

    def field(values, parity, f):
        return jnp.concatenate(
            [values[64 * h + 32 * parity + 16 * f : 64 * h + 32 * parity + 16 * f + 16] for h in range(2)],
            axis=0,
        )

    shape = (32, COLS)
    col = lax.broadcasted_iota(jnp.int32, shape, 1)
    degree_int = wave_int + core * COLS + col
    last = jnp.where(used > 0, 2 * HALF - 1, -1)
    live = degree_int <= last
    even_col = col % 2 == 0
    edge_live = wave_int + COLS - core <= last
    flows, before, after = [], [], []
    for f in range(2):
        flow = jnp.where(even_col, field(main, 0, f), field(main, 1, f))
        flow = jnp.where(live, flow, 0.0)
        border = jnp.where(core == 0, field(beside, 0, f)[:, :1], field(beside, 1, f)[:, LANES - 1 :])
        border = jnp.where(edge_live, border, 0.0)
        first = jnp.where(core == 1, border, 0.0)
        final = jnp.where(core == 0, border, 0.0)
        flows.append(flow)
        before.append(jnp.where(col == 0, first, pltpu.roll(flow, 1, 1)))
        after.append(jnp.where(col == COLS - 1, final, pltpu.roll(flow, COLS - 1, 1)))

    line = lax.broadcasted_iota(jnp.int32, (8, COLS), 1)
    degree_row = wave_int + core * COLS + line
    degree = degree_row.astype(F32)
    next_row = degree_row + 1
    squared = wave_int * wave_int
    eps_here = jnp.sqrt((degree_row * degree_row - squared).astype(F32) / (4.0 * degree * degree - 1.0))
    eps_next = jnp.sqrt(
        (next_row * next_row - squared).astype(F32) / (4.0 * (degree + 1.0) * (degree + 1.0) - 1.0)
    )
    factor = lax.rsqrt(degree * (degree + 1.0))
    low_term = ((degree + 1.0) * eps_here * factor)[:1]
    high_term = (degree * eps_next * factor)[:1]
    wave_term = (wave_int.astype(F32) * factor)[:1]
    is_real = lax.broadcasted_iota(jnp.int32, shape, 0) % 2 == 0

    def times_unit(values):
        return jnp.where(is_real, -pltpu.roll(values, 31, 0), pltpu.roll(values, 1, 0))

    vorticity = wave_term * times_unit(flows[1]) + low_term * before[0] - high_term * after[0]
    divergence = wave_term * times_unit(flows[0]) - low_term * before[1] + high_term * after[1]
    offset = wave_int - HALF + core * COLS

    @pl.when(slot == 0)
    def _():
        summed[...] = jnp.zeros_like(summed)

    for q, values in enumerate((vorticity, divergence)):
        values = jnp.where(live, values, 0.0)
        out_ref[0, q] = values.reshape(16, 2, COLS)
        wide = jnp.concatenate([values * values, jnp.zeros(shape, F32)], axis=1)
        summed[32 * q : 32 * q + 32, :] += pltpu.roll(wide, offset, 1)

    @pl.when(slot == 3)
    def _():
        for tile in range(HALF // LANES):
            split[tile] = summed[:, LANES * tile : LANES * tile + LANES]
        energy_ref[...] = jnp.concatenate(
            [
                split[tile, pl.ds(0, 32, stride=2), :] + split[tile, pl.ds(1, 32, stride=2), :]
                for tile in range(HALF // LANES)
            ],
            axis=1,
        )


def project_call(meta, data, legendre, edge):
    return pl.pallas_call(
        project_kernel,
        grid=(4,),
        out_shape=(
            jax.ShapeDtypeStruct((4, 2, 16, 2, COLS), F32),
            jax.ShapeDtypeStruct((32, HALF), F32),
        ),
        in_specs=[
            pl.BlockSpec(memory_space=pltpu.SMEM),
            pl.BlockSpec((2, 1, HALF, LANES), lambda s: (0, s // 2, 0, 0)),
            pl.BlockSpec((1, HALF, COLS), lambda s: (s, 0, 0)),
            pl.BlockSpec((1, HALF, LANES), lambda s: (s, 0, 0)),
        ],
        out_specs=(
            pl.BlockSpec((1, 2, 16, 2, COLS), lambda s: (s, 0, 0, 0, 0)),
            pl.BlockSpec((32, HALF), lambda s: (0, 0)),
        ),
        scratch_shapes=[
            pltpu.VMEM((64, HALF), F32),
            pltpu.VMEM((HALF // LANES, 64, LANES), F32),
        ],
        compiler_params=pltpu.CompilerParams(vmem_limit_bytes=VMEM_BYTES),
    )(meta, data, legendre, edge)


def reduce_kernel(energy_ref, out_ref, send_a, recv_a, send_b, recv_b, send_sems, recv_sems):
    me = lax.axis_index("wave")
    core = lax.axis_index("deg")
    plane = me // 16
    inside = me % 16

    def plane_partner(step):
        return (plane + step // 2) % 8, (core + step) % 2

    def inside_partner(step):
        return (inside + step // 2) % 16, (core + step) % 2

    barrier = pltpu.get_barrier_semaphore()

    def greet_planes(step, carry):
        there, side = plane_partner(step)
        pl.semaphore_signal(barrier, inc=1, device_id=(there * 16 + inside, side), device_id_type=MESH)
        return carry

    def greet_inside(step, carry):
        there, side = inside_partner(step)
        pl.semaphore_signal(barrier, inc=1, device_id=(plane * 16 + there, side), device_id_type=MESH)
        return carry

    lax.fori_loop(1, 16, greet_planes, 0)
    lax.fori_loop(2, 32, greet_inside, 0)
    lane = lax.broadcasted_iota(jnp.int32, (8, 3 * LANES), 1)
    for there in range(8):
        for q in range(2):
            upper = energy_ref[16 * q : 16 * q + 8, :]
            lower = energy_ref[16 * q + 8 : 16 * q + 16, :]
            upper = pltpu.roll(upper, (HALF - 160 * there) % HALF, 1)[:, : 3 * LANES]
            lower = pltpu.roll(lower, (HALF + 160 - 160 * there) % HALF, 1)[:, : 3 * LANES]
            send_a[2 * there + q] = jnp.where(lane < 160, upper, lower)
    recv_a[2 * plane + core] = send_a[2 * plane + core]
    pl.semaphore_wait(barrier, 45)

    def send_planes(step, carry):
        there, side = plane_partner(step)
        pltpu.make_async_remote_copy(
            src_ref=send_a.at[2 * there + side], dst_ref=recv_a.at[2 * plane + core],
            send_sem=send_sems.at[0], recv_sem=recv_sems.at[0],
            device_id=(there * 16 + inside, side), device_id_type=MESH,
        ).start()
        return carry

    lax.fori_loop(1, 16, send_planes, 0)
    arrived = recv_a.at[pl.ds(0, 15)]
    pltpu.make_async_copy(arrived, arrived, recv_sems.at[0]).wait()
    chunk = recv_a[0]
    for index in range(1, 16):
        chunk = chunk + recv_a[index]
    narrow = lane[:, :LANES]
    for there in range(32):
        upper = pltpu.roll(chunk, (384 - 5 * there) % 384, 1)[:, :LANES]
        lower = pltpu.roll(chunk, 384 - 96 - 5 * there, 1)[:, :LANES]
        send_b[there] = jnp.where(narrow < 64, upper, lower)
    recv_b[2 * inside + core] = send_b[2 * inside + core]

    def send_inside(step, carry):
        there, side = inside_partner(step)
        pltpu.make_async_remote_copy(
            src_ref=send_b.at[2 * there + side], dst_ref=recv_b.at[2 * inside + core],
            send_sem=send_sems.at[1], recv_sem=recv_sems.at[1],
            device_id=(plane * 16 + there, side), device_id_type=MESH,
        ).start()
        return carry

    lax.fori_loop(1, 32, send_inside, 0)
    arrived = recv_b.at[pl.ds(0, 31)]
    pltpu.make_async_copy(arrived, arrived, recv_sems.at[1]).wait()
    for q in range(2):
        chunk = recv_b[q]
        for index in range(1, 16):
            chunk = chunk + recv_b[2 * index + q]
        turned = jnp.transpose(chunk * (1.0 / ENTRIES), (1, 0))
        out_ref[:, q, :] = jnp.concatenate([turned[:5], turned[64:69]], axis=1)
    sent = send_a.at[pl.ds(0, 15)]
    pltpu.make_async_copy(sent, sent, send_sems.at[0]).wait()
    sent = send_b.at[pl.ds(0, 31)]
    pltpu.make_async_copy(sent, sent, send_sems.at[1]).wait()


def reduce_call(energy):
    vmem = pl.BlockSpec(memory_space=pltpu.VMEM)
    return pl.pallas_call(
        reduce_kernel,
        out_shape=jax.ShapeDtypeStruct((5, 2, 16), F32),
        in_specs=[vmem],
        out_specs=vmem,
        scratch_shapes=[
            pltpu.VMEM((16, 8, 3 * LANES), F32),
            pltpu.VMEM((16, 8, 3 * LANES), F32),
            pltpu.VMEM((32, 8, LANES), F32),
            pltpu.VMEM((32, 8, LANES), F32),
            pltpu.SemaphoreType.DMA((2,)),
            pltpu.SemaphoreType.DMA((2,)),
        ],
        compiler_params=pltpu.CompilerParams(collective_id=1, has_side_effects=True),
    )(energy)


def slot_numbers(owner):
    positions = jnp.arange(owner.shape[0], dtype=jnp.int32)
    same_owner = (owner[:, None] == owner[None, :]) & (positions[:, None] < positions[None, :])
    return owner * 4 + jnp.sum(same_owner.astype(jnp.int32), axis=0)


def local(wind_u, wind_v, window_m, owner, legendre):
    slot_of = slot_numbers(owner)
    here = lax.axis_index("wave") * 4 + jnp.arange(4, dtype=jnp.int32)
    hits = (slot_of[None, :] == here[:, None]).astype(jnp.int32)
    used = jnp.sum(hits, axis=1)
    wave_here = jnp.where(used > 0, jnp.sum(hits * window_m[None, :], axis=1), HALF)
    core = lax.axis_index("deg").astype(jnp.int32)
    meta = jnp.concatenate([wave_here, used, core[None]])
    outgoing = dft_call(wind_u, wind_v, window_m, slot_of)
    data, edge = exchange_call(outgoing, legendre)
    coeffs, energy = project_call(meta, data.reshape(2, 2, HALF, LANES), legendre, edge)
    spectra = reduce_call(energy).transpose(1, 2, 0)
    return (coeffs, spectra)


def solution(mesh):
    placed = (
        P("deg", None, "wave", None),
        P("deg", None, "wave", None),
        P(),
        P(),
        P("wave", None, "deg"),
    )
    return jax.shard_map(
        local,
        mesh=mesh,
        in_specs=placed,
        out_specs=(P("wave", None, None, None, "deg"), P(None, None, ("wave", "deg"))),
        check_vma=False,
    )
```

```python
import functools
import math

import jax
import jax.numpy as jnp
import numpy as np
from jax import lax
from jax.experimental import pallas as pl
from jax.experimental.pallas import tpu as pltpu
from jax.sharding import PartitionSpec as P

MESH = pl.DeviceIdType.MESH
BF16 = jnp.bfloat16
F32 = jnp.float32
VMEM_BYTES = 56 * 1024 * 1024

NLON = 5120
LANES = 128
COARSE = NLON // LANES
ENTRIES = 256
ROWS = 10
HALF = 1280
COLS = 640
CHUNK = 4

NT = (((1,), (1,)), ((), ()))


def row_order():
    source = np.arange(640).reshape(2, 2, 2, 8, ROWS)
    wanted = source.transpose(4, 1, 2, 3, 0).reshape(-1)
    return np.eye(640, dtype=np.float32)[wanted].astype(jnp.bfloat16)


def group_order():
    source = np.arange(160).reshape(ROWS, 16)
    wanted = source.transpose(1, 0).reshape(-1)
    return np.eye(160, dtype=np.float32)[wanted].astype(jnp.bfloat16)


def unit_waves(steps, window, period):
    phase = steps * window
    phase = phase - period * jnp.round(phase * (1.0 / period))
    angle = phase * (2.0 * math.pi / period)
    return jnp.cos(angle), jnp.sin(angle)


def dft_kernel(
    wind_u, wind_v, window_ref, slot_ref, order_ref, group_ref, out_ref,
    winds, coarse_cos, coarse_sin, fine_cos, fine_sin, total, split, sems,
):
    for chunk in range(COARSE // CHUNK):
        for inner in range(CHUNK):
            tile = chunk * CHUNK + inner
            for which, ref in enumerate((wind_u, wind_v)):
                pltpu.make_async_copy(ref.at[:, tile], winds.at[tile, which], sems.at[chunk]).start()
    window = window_ref[...].astype(F32)
    coarse_steps = lax.broadcasted_iota(jnp.int32, (COARSE, ENTRIES), 0).astype(F32)
    fine_steps = lax.broadcasted_iota(jnp.int32, (LANES, ENTRIES), 0).astype(F32)
    cos_part, sin_part = unit_waves(coarse_steps, window, float(COARSE))
    coarse_cos[...] = cos_part
    coarse_sin[...] = sin_part
    cos_part, sin_part = unit_waves(fine_steps, window, float(NLON))
    fine_cos[...] = cos_part * (1.0 / NLON)
    fine_sin[...] = sin_part * (1.0 / NLON)
    total[...] = jnp.zeros_like(total)

    def step(chunk, carry):
        part = winds.at[pl.ds(chunk * CHUNK, CHUNK)]
        pltpu.make_async_copy(part, part, sems.at[chunk]).wait()
        cos_b = fine_cos[...]
        sin_b = fine_sin[...]
        highs, lows, pieces = [], [], []
        for inner in range(CHUNK):
            tile = chunk * CHUNK + inner
            cos_a = coarse_cos[pl.ds(tile, 1), :]
            sin_a = coarse_sin[pl.ds(tile, 1), :]
            table = jnp.concatenate(
                [cos_a * cos_b - sin_a * sin_b, -(sin_a * cos_b + cos_a * sin_b)], axis=1
            )
            high = table.astype(BF16)
            highs.append(high)
            lows.append((table - high.astype(F32)).astype(BF16))
            pieces.append(winds.at[tile].reshape(320, LANES)[...])
        data = jnp.concatenate(pieces, axis=1)
        total[...] += jnp.dot(
            data, jnp.concatenate(highs, axis=0), preferred_element_type=F32
        ) + jnp.dot(data, jnp.concatenate(lows, axis=0), preferred_element_type=F32)
        return carry

    lax.fori_loop(0, COARSE // CHUNK, step, 0)
    for tile in range(4):
        split[tile] = total[:, LANES * tile : LANES * tile + LANES]

    def hemisphere(h):
        return jnp.concatenate([split[tile, pl.ds(h, 160, stride=2), :] for tile in range(4)], axis=1)

    north = hemisphere(0)
    south = hemisphere(1)
    even = (north + south).astype(BF16)
    odd = (north - south).astype(BF16)
    paired = jnp.concatenate(
        [even[:, :ENTRIES], odd[:, :ENTRIES], even[:, ENTRIES:], odd[:, ENTRIES:]], axis=0
    )
    ordered = jnp.dot(order_ref[...], paired, preferred_element_type=F32).astype(BF16)
    empty = jnp.zeros((64, ENTRIES), BF16)
    blocks = []
    for row in range(ROWS):
        block = ordered[64 * row : 64 * row + 64]
        blocks.append(jnp.concatenate([block, empty], axis=1))
        blocks.append(jnp.concatenate([empty, block], axis=1))
    blocks = jnp.concatenate(blocks, axis=0)
    pair_ids = 2 * lax.broadcasted_iota(jnp.int32, (256, ENTRIES), 0)
    slots = slot_ref[...]
    placing = jnp.concatenate(
        [
            (slots == pair_ids).astype(F32).astype(BF16),
            (slots == pair_ids + 1).astype(F32).astype(BF16),
        ],
        axis=1,
    )
    placed = lax.dot_general(placing, blocks, NT, preferred_element_type=F32).astype(BF16)
    stacked = jnp.concatenate(
        [
            jnp.concatenate(
                [placed[16 * g : 16 * g + 16, LANES * row : LANES * row + LANES] for g in range(16)],
                axis=1,
            )
            for row in range(ROWS)
        ],
        axis=0,
    )
    result = jnp.dot(group_ref[...], stacked, preferred_element_type=F32).astype(BF16)
    for g in range(16):
        out_ref[160 * g : 160 * g + 160, :] = result[:, LANES * g : LANES * g + LANES]


def dft_call(wind_u, wind_v, window_m, slot_of):
    vmem = pl.BlockSpec(memory_space=pltpu.VMEM)
    hbm = pl.BlockSpec(memory_space=pl.ANY)

    def tiles(wind):
        split = wind.transpose(0, 2, 1, 3).reshape(8, ROWS, 2, COARSE, LANES)
        return split.transpose(0, 1, 3, 2, 4).reshape(80, COARSE, 2, LANES)

    return pl.pallas_call(
        dft_kernel,
        out_shape=jax.ShapeDtypeStruct((2560, LANES), BF16),
        in_specs=[hbm, hbm, vmem, vmem, vmem, vmem],
        out_specs=vmem,
        scratch_shapes=[
            pltpu.VMEM((COARSE, 2, 80, 2, LANES), BF16),
            pltpu.VMEM((COARSE, ENTRIES), F32),
            pltpu.VMEM((COARSE, ENTRIES), F32),
            pltpu.VMEM((LANES, ENTRIES), F32),
            pltpu.VMEM((LANES, ENTRIES), F32),
            pltpu.VMEM((320, 2 * ENTRIES), F32),
            pltpu.VMEM((4, 320, LANES), F32),
            pltpu.SemaphoreType.DMA((COARSE // CHUNK,)),
        ],
        compiler_params=pltpu.CompilerParams(vmem_limit_bytes=VMEM_BYTES),
    )(
        tiles(wind_u), tiles(wind_v), window_m[None, :], slot_of[None, :],
        jnp.asarray(row_order()), jnp.asarray(group_order()),
    )


def exchange_kernel(
    send_ref, table_ref, data_ref, edge_ref,
    send_sem, recv_sem, core_send, core_recv, edge_send, edge_recv, meet_x, meet_y,
):
    me = lax.axis_index("wave")
    core = lax.axis_index("deg")
    other = 1 - core
    plane = me // 16
    inside = me % 16

    row = inside // 4
    column = inside % 4

    def partner(step):
        turn = step % 8
        away = (4 + (turn + 1) // 2 * (1 - 2 * (turn % 2)) + 8) % 8
        return (plane + away) % 8 * 16 + (row + step // 32) % 4 * 4 + (column + step // 8) % 4

    def along_z(step):
        return (plane + step) % 8 * 16 + inside

    def along_x(step):
        return plane * 16 + (row + step) % 4 * 4 + column

    def along_y(step):
        return plane * 16 + row * 4 + (column + step) % 4

    def greet(sem, where, count):
        for step in range(1, count):
            pl.semaphore_signal(sem, inc=1, device_id=(where(step), core), device_id_type=MESH)

    barrier = pltpu.get_barrier_semaphore()
    greet(barrier, along_z, 8)
    greet(barrier, along_x, 4)
    greet(barrier, along_y, 4)
    pl.semaphore_signal(barrier, inc=1, device_id=(me, other), device_id_type=MESH)
    pl.semaphore_wait(barrier, 14)
    greet(meet_x, along_x, 4)
    pl.semaphore_wait(meet_x, 3)
    greet(meet_y, along_y, 4)
    pl.semaphore_wait(meet_y, 3)

    edge = pltpu.make_async_remote_copy(
        src_ref=table_ref.at[:, :, pl.ds(pl.multiple_of(other * 512, LANES), LANES)],
        dst_ref=edge_ref, send_sem=edge_send, recv_sem=edge_recv,
        device_id=(me, other), device_id_type=MESH,
    )
    own = pltpu.make_async_copy(send_ref.at[me], data_ref.at[core, :, plane, inside], recv_sem.at[0])
    own.start()

    def send(step, carry):
        target = partner(step)
        pltpu.make_async_remote_copy(
            src_ref=send_ref.at[target], dst_ref=data_ref.at[core, :, plane, inside],
            send_sem=send_sem, recv_sem=recv_sem.at[step // 8],
            device_id=(target, core), device_id_type=MESH,
        ).start()
        return carry

    lax.fori_loop(0, 7, send, 0)
    lax.fori_loop(8, 128, send, 0)
    edge.start()

    def forward(step):
        source = (row + 4 - step // 4) % 4 * 4 + (column + 16 - step) % 4
        part = data_ref.at[core, :, :, source]
        return source, part, pltpu.make_async_remote_copy(
            src_ref=part, dst_ref=part, send_sem=core_send.at[step], recv_sem=core_recv.at[step],
            device_id=(me, other), device_id_type=MESH,
        )

    for step in range(16):
        source, part, copy = forward(step)
        pltpu.make_async_copy(part, part, recv_sem.at[step]).wait()
        copy.start()
    for step in range(16):
        source, part, copy = forward(step)
        copy.wait_send()
        arrived = data_ref.at[other, :, :, source]
        pltpu.make_async_copy(arrived, arrived, core_recv.at[step]).wait()
    edge.wait()
    sent = send_ref.at[pl.ds(0, 127)]
    pltpu.make_async_copy(sent, sent, send_sem).wait()


def exchange_call(outgoing, legendre):
    hbm = pl.BlockSpec(memory_space=pl.ANY)
    dma = pltpu.SemaphoreType.DMA
    return pl.pallas_call(
        exchange_kernel,
        out_shape=(
            jax.ShapeDtypeStruct((2, 2, 8, 16, 5, 2, LANES), BF16),
            jax.ShapeDtypeStruct((4, HALF, LANES), BF16),
        ),
        in_specs=[hbm, hbm],
        out_specs=(hbm, hbm),
        scratch_shapes=[
            dma, dma((16,)), dma((16,)), dma((16,)), dma, dma,
            pltpu.SemaphoreType.REGULAR, pltpu.SemaphoreType.REGULAR,
        ],
        compiler_params=pltpu.CompilerParams(
            collective_id=0, has_side_effects=True, vmem_limit_bytes=VMEM_BYTES
        ),
    )(outgoing.reshape(128, 2, 5, 2, LANES), legendre)


def project_kernel(meta, data_ref, table_ref, edge_ref, out_ref, energy_ref, summed, split):
    slot = pl.program_id(0)
    core = meta[8]
    wave_int = meta[slot]
    used = meta[4 + slot]
    half = slot % 2
    row_ids = lax.broadcasted_iota(jnp.int32, (64, LANES), 0)
    col_ids = lax.broadcasted_iota(jnp.int32, (64, LANES), 1)
    picking = (col_ids == row_ids + 64 * half).astype(F32).astype(BF16)
    rows = jnp.concatenate(
        [
            lax.dot_general(picking, data_ref[h, 0], NT, preferred_element_type=F32).astype(BF16)
            for h in range(2)
        ],
        axis=0,
    )
    main = jnp.dot(rows, table_ref[0], preferred_element_type=F32)
    beside = jnp.dot(rows, edge_ref[0], preferred_element_type=F32)

    def field(values, parity, f):
        return jnp.concatenate(
            [values[64 * h + 32 * parity + 16 * f : 64 * h + 32 * parity + 16 * f + 16] for h in range(2)],
            axis=0,
        )

    shape = (32, COLS)
    col = lax.broadcasted_iota(jnp.int32, shape, 1)
    degree_int = wave_int + core * COLS + col
    last = jnp.where(used > 0, 2 * HALF - 1, -1)
    live = degree_int <= last
    even_col = col % 2 == 0
    edge_live = wave_int + COLS - core <= last
    flows, before, after = [], [], []
    for f in range(2):
        flow = jnp.where(even_col, field(main, 0, f), field(main, 1, f))
        flow = jnp.where(live, flow, 0.0)
        border = jnp.where(core == 0, field(beside, 0, f)[:, :1], field(beside, 1, f)[:, LANES - 1 :])
        border = jnp.where(edge_live, border, 0.0)
        first = jnp.where(core == 1, border, 0.0)
        final = jnp.where(core == 0, border, 0.0)
        flows.append(flow)
        before.append(jnp.where(col == 0, first, pltpu.roll(flow, 1, 1)))
        after.append(jnp.where(col == COLS - 1, final, pltpu.roll(flow, COLS - 1, 1)))

    line = lax.broadcasted_iota(jnp.int32, (8, COLS), 1)
    degree_row = wave_int + core * COLS + line
    degree = degree_row.astype(F32)
    next_row = degree_row + 1
    squared = wave_int * wave_int
    eps_here = jnp.sqrt((degree_row * degree_row - squared).astype(F32) / (4.0 * degree * degree - 1.0))
    eps_next = jnp.sqrt(
        (next_row * next_row - squared).astype(F32) / (4.0 * (degree + 1.0) * (degree + 1.0) - 1.0)
    )
    factor = lax.rsqrt(degree * (degree + 1.0))
    low_term = ((degree + 1.0) * eps_here * factor)[:1]
    high_term = (degree * eps_next * factor)[:1]
    wave_term = (wave_int.astype(F32) * factor)[:1]
    is_real = lax.broadcasted_iota(jnp.int32, shape, 0) % 2 == 0

    def times_unit(values):
        return jnp.where(is_real, -pltpu.roll(values, 31, 0), pltpu.roll(values, 1, 0))

    vorticity = wave_term * times_unit(flows[1]) + low_term * before[0] - high_term * after[0]
    divergence = wave_term * times_unit(flows[0]) - low_term * before[1] + high_term * after[1]
    offset = wave_int - HALF + core * COLS

    @pl.when(slot == 0)
    def _():
        summed[...] = jnp.zeros_like(summed)

    for q, values in enumerate((vorticity, divergence)):
        values = jnp.where(live, values, 0.0)
        out_ref[0, q] = values.reshape(16, 2, COLS)
        wide = jnp.concatenate([values * values, jnp.zeros(shape, F32)], axis=1)
        summed[32 * q : 32 * q + 32, :] += pltpu.roll(wide, offset, 1)

    @pl.when(slot == 3)
    def _():
        for tile in range(HALF // LANES):
            split[tile] = summed[:, LANES * tile : LANES * tile + LANES]
        energy_ref[...] = jnp.concatenate(
            [
                split[tile, pl.ds(0, 32, stride=2), :] + split[tile, pl.ds(1, 32, stride=2), :]
                for tile in range(HALF // LANES)
            ],
            axis=1,
        )


def project_call(meta, data, legendre, edge):
    return pl.pallas_call(
        project_kernel,
        grid=(4,),
        out_shape=(
            jax.ShapeDtypeStruct((4, 2, 16, 2, COLS), F32),
            jax.ShapeDtypeStruct((32, HALF), F32),
        ),
        in_specs=[
            pl.BlockSpec(memory_space=pltpu.SMEM),
            pl.BlockSpec((2, 1, HALF, LANES), lambda s: (0, s // 2, 0, 0)),
            pl.BlockSpec((1, HALF, COLS), lambda s: (s, 0, 0)),
            pl.BlockSpec((1, HALF, LANES), lambda s: (s, 0, 0)),
        ],
        out_specs=(
            pl.BlockSpec((1, 2, 16, 2, COLS), lambda s: (s, 0, 0, 0, 0)),
            pl.BlockSpec((32, HALF), lambda s: (0, 0)),
        ),
        scratch_shapes=[
            pltpu.VMEM((64, HALF), F32),
            pltpu.VMEM((HALF // LANES, 64, LANES), F32),
        ],
        compiler_params=pltpu.CompilerParams(vmem_limit_bytes=VMEM_BYTES),
    )(meta, data, legendre, edge)


def reduce_kernel(energy_ref, out_ref, send_a, recv_a, send_b, recv_b, send_sems, recv_sems):
    me = lax.axis_index("wave")
    core = lax.axis_index("deg")
    plane = me // 16
    inside = me % 16

    def plane_partner(step):
        return (plane + step // 2) % 8, (core + step) % 2

    def inside_partner(step):
        return (inside + step // 2) % 16, (core + step) % 2

    barrier = pltpu.get_barrier_semaphore()

    def greet_planes(step, carry):
        there, side = plane_partner(step)
        pl.semaphore_signal(barrier, inc=1, device_id=(there * 16 + inside, side), device_id_type=MESH)
        return carry

    def greet_inside(step, carry):
        there, side = inside_partner(step)
        pl.semaphore_signal(barrier, inc=1, device_id=(plane * 16 + there, side), device_id_type=MESH)
        return carry

    lax.fori_loop(1, 16, greet_planes, 0)
    lax.fori_loop(2, 32, greet_inside, 0)
    lane = lax.broadcasted_iota(jnp.int32, (8, 3 * LANES), 1)
    for there in range(8):
        for q in range(2):
            upper = energy_ref[16 * q : 16 * q + 8, :]
            lower = energy_ref[16 * q + 8 : 16 * q + 16, :]
            upper = pltpu.roll(upper, (HALF - 160 * there) % HALF, 1)[:, : 3 * LANES]
            lower = pltpu.roll(lower, (HALF + 160 - 160 * there) % HALF, 1)[:, : 3 * LANES]
            send_a[2 * there + q] = jnp.where(lane < 160, upper, lower)
    recv_a[2 * plane + core] = send_a[2 * plane + core]
    pl.semaphore_wait(barrier, 45)

    def send_planes(step, carry):
        there, side = plane_partner(step)
        pltpu.make_async_remote_copy(
            src_ref=send_a.at[2 * there + side], dst_ref=recv_a.at[2 * plane + core],
            send_sem=send_sems.at[0], recv_sem=recv_sems.at[0],
            device_id=(there * 16 + inside, side), device_id_type=MESH,
        ).start()
        return carry

    lax.fori_loop(1, 16, send_planes, 0)
    arrived = recv_a.at[pl.ds(0, 15)]
    pltpu.make_async_copy(arrived, arrived, recv_sems.at[0]).wait()
    chunk = recv_a[0]
    for index in range(1, 16):
        chunk = chunk + recv_a[index]
    narrow = lane[:, :LANES]
    for there in range(32):
        upper = pltpu.roll(chunk, (384 - 5 * there) % 384, 1)[:, :LANES]
        lower = pltpu.roll(chunk, 384 - 96 - 5 * there, 1)[:, :LANES]
        send_b[there] = jnp.where(narrow < 64, upper, lower)
    recv_b[2 * inside + core] = send_b[2 * inside + core]

    def send_inside(step, carry):
        there, side = inside_partner(step)
        pltpu.make_async_remote_copy(
            src_ref=send_b.at[2 * there + side], dst_ref=recv_b.at[2 * inside + core],
            send_sem=send_sems.at[1], recv_sem=recv_sems.at[1],
            device_id=(plane * 16 + there, side), device_id_type=MESH,
        ).start()
        return carry

    lax.fori_loop(1, 32, send_inside, 0)
    arrived = recv_b.at[pl.ds(0, 31)]
    pltpu.make_async_copy(arrived, arrived, recv_sems.at[1]).wait()
    for q in range(2):
        chunk = recv_b[q]
        for index in range(1, 16):
            chunk = chunk + recv_b[2 * index + q]
        turned = jnp.transpose(chunk * (1.0 / ENTRIES), (1, 0))
        out_ref[:, q, :] = jnp.concatenate([turned[:5], turned[64:69]], axis=1)
    sent = send_a.at[pl.ds(0, 15)]
    pltpu.make_async_copy(sent, sent, send_sems.at[0]).wait()
    sent = send_b.at[pl.ds(0, 31)]
    pltpu.make_async_copy(sent, sent, send_sems.at[1]).wait()


def reduce_call(energy):
    vmem = pl.BlockSpec(memory_space=pltpu.VMEM)
    return pl.pallas_call(
        reduce_kernel,
        out_shape=jax.ShapeDtypeStruct((5, 2, 16), F32),
        in_specs=[vmem],
        out_specs=vmem,
        scratch_shapes=[
            pltpu.VMEM((16, 8, 3 * LANES), F32),
            pltpu.VMEM((16, 8, 3 * LANES), F32),
            pltpu.VMEM((32, 8, LANES), F32),
            pltpu.VMEM((32, 8, LANES), F32),
            pltpu.SemaphoreType.DMA((2,)),
            pltpu.SemaphoreType.DMA((2,)),
        ],
        compiler_params=pltpu.CompilerParams(collective_id=1, has_side_effects=True),
    )(energy)


def slot_numbers(owner):
    positions = jnp.arange(owner.shape[0], dtype=jnp.int32)
    same_owner = (owner[:, None] == owner[None, :]) & (positions[:, None] < positions[None, :])
    return owner * 4 + jnp.sum(same_owner.astype(jnp.int32), axis=0)


def local(wind_u, wind_v, window_m, owner, legendre):
    slot_of = slot_numbers(owner)
    here = lax.axis_index("wave") * 4 + jnp.arange(4, dtype=jnp.int32)
    hits = (slot_of[None, :] == here[:, None]).astype(jnp.int32)
    used = jnp.sum(hits, axis=1)
    wave_here = jnp.where(used > 0, jnp.sum(hits * window_m[None, :], axis=1), HALF)
    core = lax.axis_index("deg").astype(jnp.int32)
    meta = jnp.concatenate([wave_here, used, core[None]])
    outgoing = dft_call(wind_u, wind_v, window_m, slot_of)
    data, edge = exchange_call(outgoing, legendre)
    coeffs, energy = project_call(meta, data.reshape(2, 2, HALF, LANES), legendre, edge)
    spectra = reduce_call(energy).transpose(1, 2, 0)
    return (coeffs, spectra)


def solution(mesh):
    placed = (
        P("deg", None, "wave", None),
        P("deg", None, "wave", None),
        P(),
        P(),
        P("wave", None, "deg"),
    )
    return jax.shard_map(
        local,
        mesh=mesh,
        in_specs=placed,
        out_specs=(P("wave", None, None, None, "deg"), P(None, None, ("wave", "deg"))),
        check_vma=False,
    )
```

```python
import math

import jax
import jax.numpy as jnp
from jax import lax
from jax.experimental import pallas as pl
from jax.experimental.pallas import tpu as pltpu
from jax.sharding import PartitionSpec as P

MESH = pl.DeviceIdType.MESH
BF16 = jnp.bfloat16
F32 = jnp.float32
I32 = jnp.int32
VMEM_BYTES = 56 * 1024 * 1024

NLON = 5120
LANES = 128
COARSE = NLON // LANES
ENTRIES = 256
ROWS = 10
HALF = 1280
COLS = 640
WIDE = COLS + LANES
CHUNK = 4
STEPS = COARSE // CHUNK

NT = (((1,), (1,)), ((), ()))


def iota(shape, axis):
    return lax.broadcasted_iota(I32, shape, axis)


def one_hot(hits):
    return hits.astype(F32).astype(BF16)


def row_order():
    wanted = iota((320, 320), 0)
    source = wanted % 2 * 160 + wanted // 16 % 2 * 80 + wanted // 2 % 8 * 10 + wanted // 32
    return one_hot(source == iota((320, 320), 1))


def group_order():
    source = iota((160, 160), 1)
    return one_hot(source % 16 * ROWS + source // 16 == iota((160, 160), 0))


def unit_waves(count, window, period):
    phase = iota((count, ENTRIES), 0).astype(F32) * window
    phase = phase - period * jnp.round(phase * (1.0 / period))
    angle = phase * (2.0 * math.pi / period)
    return jnp.cos(angle), jnp.sin(angle)


def stack(pieces, axis):
    return jnp.concatenate(pieces, axis=axis)


def kernel(
    wind_u, wind_v, window_ref, owner_ref, table_hbm, coeffs_hbm, spectra_ref,
    winds, coarse_cos, coarse_sin, fine_cos, fine_sin, highs, lows, total, split,
    outgoing, data, table, projected, coeffs, summed, send_a, recv_a, send_b, recv_b,
    wind_sems, table_sems, edge_sems, meet_core, meet_x, meet_y,
    out_sems, in_sems, core_send, core_recv, coeffs_sems, fold_send, fold_recv,
):
    me = lax.axis_index("wave")
    core = lax.axis_index("deg")
    other = 1 - core
    plane = me // 16
    inside = me % 16
    row = inside // 4
    column = inside % 4

    def along_z(step):
        return (plane + step) % 8 * 16 + inside

    def along_x(step):
        return plane * 16 + (row + step) % 4 * 4 + column

    def along_y(step):
        return plane * 16 + row * 4 + (column + step) % 4

    def signal(sem, where, side):
        pl.semaphore_signal(sem, inc=1, device_id=(where, side), device_id_type=MESH)

    def greet(sem, where, count):
        for step in range(1, count):
            signal(sem, where(step), core)

    barrier = pltpu.get_barrier_semaphore()
    greet(barrier, along_z, 8)
    greet(barrier, along_x, 4)
    greet(barrier, along_y, 4)
    signal(barrier, me, other)

    for f, ref in enumerate((wind_u, wind_v)):
        for tile in range(COARSE):
            pltpu.make_async_copy(ref.at[:, tile], winds.at[f, tile], wind_sems.at[f, tile // CHUNK]).start()

    def table_copy(slot):
        return pltpu.make_async_copy(
            table_hbm.at[slot], table.at[slot, :, pl.ds(0, COLS)], table_sems.at[slot]
        )

    for slot in range(4):
        table_copy(slot).start()

    window = window_ref[...].astype(F32)
    owner = owner_ref[...].astype(F32)
    owner_rows = jnp.broadcast_to(owner, (ENTRIES, ENTRIES))
    same = (jnp.transpose(owner_rows, (1, 0)) == owner_rows) & (
        iota((ENTRIES, ENTRIES), 0) < iota((ENTRIES, ENTRIES), 1)
    )
    rank = jnp.sum(same.astype(F32), axis=0, keepdims=True)
    placing = one_hot(owner_ref[...] == iota((128, ENTRIES), 0))
    rank_masks = [one_hot(rank == float(slot)) for slot in range(4)]

    cos_part, sin_part = unit_waves(COARSE, window, float(COARSE))
    coarse_cos[...] = cos_part
    coarse_sin[...] = sin_part
    cos_part, sin_part = unit_waves(LANES, window, float(NLON))
    fine_cos[...] = cos_part * (1.0 / NLON)
    fine_sin[...] = sin_part * (1.0 / NLON)

    def wind_chunk(f, chunk):
        part = winds.at[f, pl.ds(chunk * CHUNK, CHUNK)]
        pltpu.make_async_copy(part, part, wind_sems.at[f, chunk]).wait()
        return stack(
            [winds.at[f, chunk * CHUNK + inner].reshape(160, LANES)[...] for inner in range(CHUNK)], 1
        )

    def first_step(chunk, carry):
        cos_b = fine_cos[...]
        sin_b = fine_sin[...]
        for inner in range(CHUNK):
            tile = chunk * CHUNK + inner
            cos_a = coarse_cos[pl.ds(tile, 1), :]
            sin_a = coarse_sin[pl.ds(tile, 1), :]
            values = stack([cos_a * cos_b - sin_a * sin_b, -(sin_a * cos_b + cos_a * sin_b)], 1)
            high = values.astype(BF16)
            highs[chunk, LANES * inner : LANES * inner + LANES, :] = high
            lows[chunk, LANES * inner : LANES * inner + LANES, :] = (values - high.astype(F32)).astype(BF16)
        return second_step(0, chunk, carry)

    def second_step(f, chunk, carry):
        part = wind_chunk(f, chunk)
        total[...] += jnp.dot(part, highs[chunk], preferred_element_type=F32) + jnp.dot(
            part, lows[chunk], preferred_element_type=F32
        )
        return carry

    def publish(f):
        for tile in range(4):
            split[tile, :160] = total[:, LANES * tile : LANES * tile + LANES]
        north = stack([split[tile, pl.ds(0, 80, stride=2), :] for tile in range(4)], 1)
        south = stack([split[tile, pl.ds(1, 80, stride=2), :] for tile in range(4)], 1)
        even = (north + south).astype(BF16)
        odd = (north - south).astype(BF16)
        paired = stack([even[:, :ENTRIES], odd[:, :ENTRIES], even[:, ENTRIES:], odd[:, ENTRIES:]], 0)
        ordered = jnp.dot(row_order(), paired, preferred_element_type=F32).astype(BF16)
        blocks = stack(
            [
                ordered[32 * line : 32 * line + 32] * rank_masks[slot]
                for line in range(ROWS)
                for slot in range(4)
            ],
            0,
        )
        placed = lax.dot_general(placing, blocks, NT, preferred_element_type=F32).astype(BF16)
        stacked = stack(
            [
                stack(
                    [placed[16 * g : 16 * g + 16, LANES * line : LANES * line + LANES] for g in range(8)], 1
                )
                for line in range(ROWS)
            ],
            0,
        )
        result = jnp.dot(group_order(), stacked, preferred_element_type=F32).astype(BF16)
        flat = outgoing.at[f].reshape(HALF, LANES)
        for g in range(8):
            flat[160 * g : 160 * g + 160, :] = result[:, LANES * g : LANES * g + LANES]

    def partner(step):
        turn = step % 8
        away = (4 + (turn + 1) // 2 * (1 - 2 * (turn % 2)) + 8) % 8
        return (plane + away) % 8 * 16 + (row + step // 32) % 4 * 4 + (column + step // 8) % 4

    def own_copy(f):
        return pltpu.make_async_copy(
            outgoing.at[f, me], data.at[f, core, plane, inside], in_sems.at[f, 0]
        )

    def send_all(f):
        own_copy(f).start()

        def send(step, carry):
            target = partner(step)
            pltpu.make_async_remote_copy(
                src_ref=outgoing.at[f, target], dst_ref=data.at[f, core, plane, inside],
                send_sem=out_sems.at[f], recv_sem=in_sems.at[f, step // 8],
                device_id=(target, core), device_id_type=MESH,
            ).start()
            return carry

        lax.fori_loop(0, 7, send, 0)
        lax.fori_loop(8, 128, send, 0)

    def source_of(step):
        return (row + 4 - step // 4) % 4 * 4 + (column + 16 - step) % 4

    def forward(f, step):
        part = data.at[f, core, :, source_of(step)]
        return pltpu.make_async_remote_copy(
            src_ref=part, dst_ref=part, send_sem=core_send.at[f, step], recv_sem=core_recv.at[f, step],
            device_id=(me, other), device_id_type=MESH,
        )

    def forward_all(f):
        for step in range(16):
            part = data.at[f, core, :, source_of(step)]
            pltpu.make_async_copy(part, part, in_sems.at[f, step]).wait()
            forward(f, step).start()
        for step in range(16):
            arrived = data.at[f, other, :, source_of(step)]
            pltpu.make_async_copy(arrived, arrived, core_recv.at[f, step]).wait()

    unit = one_hot(iota((LANES, LANES), 0) == iota((LANES, LANES), 1))

    def project(f):
        turned = [
            lax.dot_general(
                unit, data.at[f, h].reshape(HALF, LANES)[...], NT, preferred_element_type=F32
            ).astype(BF16)
            for h in range(2)
        ]
        results = []
        for slot in range(4):
            if f == 0:
                table_copy(slot).wait()
            rows = stack([turned[h][32 * slot : 32 * slot + 32] for h in range(2)], 0)
            results.append(jnp.dot(rows, table[slot], preferred_element_type=F32))
        return results

    total[...] = jnp.zeros_like(total)
    lax.fori_loop(0, 4, first_step, 0)
    pl.semaphore_wait(barrier, 14)
    signal(meet_core, me, other)
    edge = pltpu.make_async_remote_copy(
        src_ref=table_hbm.at[:, :, pl.ds(pl.multiple_of(other * 512, LANES), LANES)],
        dst_ref=table.at[:, :, pl.ds(COLS, LANES)],
        send_sem=edge_sems.at[0], recv_sem=edge_sems.at[1],
        device_id=(me, other), device_id_type=MESH,
    )
    lax.fori_loop(4, 7, first_step, 0)
    pl.semaphore_wait(meet_core, 1)
    greet(meet_x, along_x, 4)
    lax.fori_loop(7, STEPS, first_step, 0)
    pl.semaphore_wait(meet_x, 3)
    greet(meet_y, along_y, 4)
    publish(0)
    pl.semaphore_wait(meet_y, 3)
    send_all(0)
    edge.start()

    total[...] = jnp.zeros_like(total)
    lax.fori_loop(0, STEPS, lambda chunk, carry: second_step(1, chunk, carry), 0)
    publish(1)
    send_all(1)

    forward_all(0)
    edge.wait()
    for slot, values in enumerate(project(0)):
        projected[slot] = values
    forward_all(1)
    second = project(1)

    shape = (32, COLS)
    col = iota(shape, 1)
    even_col = col % 2 == 0
    is_real = iota(shape, 0) % 2 == 0

    def times_unit(values):
        return jnp.where(is_real, -pltpu.roll(values, 31, 0), pltpu.roll(values, 1, 0))

    summed[...] = jnp.zeros_like(summed)
    for slot in range(4):
        hits = ((owner_ref[...] == me) & (rank == float(slot))).astype(F32)
        used = jnp.sum(hits)
        wave = jnp.where(used > 0, jnp.sum(hits * window), float(HALF)).astype(I32)
        last = jnp.where(used > 0, 2 * HALF - 1, -1)
        first_degree = wave + core * COLS
        live = first_degree + col <= last
        edge_live = wave + COLS - core <= last
        flows, before, after = [], [], []
        for values in (projected[slot], second[slot]):
            even = stack([values[0:16], values[32:48]], 0)
            odd = stack([values[16:32], values[48:64]], 0)
            flow = jnp.where(even_col, even[:, :COLS], odd[:, :COLS])
            flow = jnp.where(live, flow, 0.0)
            border = jnp.where(core == 0, even[:, COLS : COLS + 1], odd[:, WIDE - 1 :])
            border = jnp.where(edge_live, border, 0.0)
            flows.append(flow)
            before.append(
                jnp.where(col == 0, jnp.where(core == 1, border, 0.0), pltpu.roll(flow, 1, 1))
            )
            after.append(
                jnp.where(col == COLS - 1, jnp.where(core == 0, border, 0.0), pltpu.roll(flow, COLS - 1, 1))
            )
        degree_row = first_degree + iota((8, COLS), 1)
        degree = degree_row.astype(F32)
        next_row = degree_row + 1
        squared = wave * wave
        eps_here = jnp.sqrt((degree_row * degree_row - squared).astype(F32) / (4.0 * degree * degree - 1.0))
        eps_next = jnp.sqrt(
            (next_row * next_row - squared).astype(F32) / (4.0 * (degree + 1.0) * (degree + 1.0) - 1.0)
        )
        factor = lax.rsqrt(degree * (degree + 1.0))
        low_term = ((degree + 1.0) * eps_here * factor)[:1]
        high_term = (degree * eps_next * factor)[:1]
        wave_term = (wave.astype(F32) * factor)[:1]
        vorticity = wave_term * times_unit(flows[1]) + low_term * before[0] - high_term * after[0]
        divergence = wave_term * times_unit(flows[0]) - low_term * before[1] + high_term * after[1]
        for q, values in enumerate((vorticity, divergence)):
            values = jnp.where(live, values, 0.0)
            coeffs[slot, q] = values.reshape(16, 2, COLS)
            wide = stack([values * values, jnp.zeros(shape, F32)], 1)
            summed[32 * q : 32 * q + 32, :] += pltpu.roll(wide, first_degree - HALF, 1)
        pltpu.make_async_copy(coeffs.at[slot], coeffs_hbm.at[slot], coeffs_sems.at[slot]).start()

    for tile in range(HALF // LANES):
        base = 64 * (tile // 4)
        split[tile % 4, base : base + 64] = summed[:, LANES * tile : LANES * tile + LANES]
    pieces = []
    for tile in range(HALF // LANES):
        base = 64 * (tile // 4)
        pieces.append(
            split[tile % 4, pl.ds(base, 32, stride=2), :] + split[tile % 4, pl.ds(base + 1, 32, stride=2), :]
        )
    energy = stack(pieces, 1)

    def plane_partner(step):
        return (plane + step // 2) % 8, (core + step) % 2

    def inside_partner(step):
        return (inside + step // 2) % 16, (core + step) % 2

    lane = iota((8, 3 * LANES), 1)
    for there in range(8):
        for q in range(2):
            upper = energy[16 * q : 16 * q + 8, :]
            lower = energy[16 * q + 8 : 16 * q + 16, :]
            upper = pltpu.roll(upper, (HALF - 160 * there) % HALF, 1)[:, : 3 * LANES]
            lower = pltpu.roll(lower, (HALF + 160 - 160 * there) % HALF, 1)[:, : 3 * LANES]
            send_a[2 * there + q] = jnp.where(lane < 160, upper, lower)
    recv_a[2 * plane + core] = send_a[2 * plane + core]

    def send_planes(step, carry):
        there, side = plane_partner(step)
        pltpu.make_async_remote_copy(
            src_ref=send_a.at[2 * there + side], dst_ref=recv_a.at[2 * plane + core],
            send_sem=fold_send.at[0], recv_sem=fold_recv.at[0],
            device_id=(there * 16 + inside, side), device_id_type=MESH,
        ).start()
        return carry

    lax.fori_loop(1, 16, send_planes, 0)
    arrived = recv_a.at[pl.ds(0, 15)]
    pltpu.make_async_copy(arrived, arrived, fold_recv.at[0]).wait()
    chunk = recv_a[0]
    for index in range(1, 16):
        chunk = chunk + recv_a[index]
    narrow = lane[:, :LANES]
    for there in range(32):
        upper = pltpu.roll(chunk, (384 - 5 * there) % 384, 1)[:, :LANES]
        lower = pltpu.roll(chunk, 384 - 96 - 5 * there, 1)[:, :LANES]
        send_b[there] = jnp.where(narrow < 64, upper, lower)
    recv_b[2 * inside + core] = send_b[2 * inside + core]

    def send_inside(step, carry):
        there, side = inside_partner(step)
        pltpu.make_async_remote_copy(
            src_ref=send_b.at[2 * there + side], dst_ref=recv_b.at[2 * inside + core],
            send_sem=fold_send.at[1], recv_sem=fold_recv.at[1],
            device_id=(plane * 16 + there, side), device_id_type=MESH,
        ).start()
        return carry

    lax.fori_loop(1, 32, send_inside, 0)
    arrived = recv_b.at[pl.ds(0, 31)]
    pltpu.make_async_copy(arrived, arrived, fold_recv.at[1]).wait()
    for q in range(2):
        chunk = recv_b[q]
        for index in range(1, 16):
            chunk = chunk + recv_b[2 * index + q]
        turned = jnp.transpose(chunk * (1.0 / ENTRIES), (1, 0))
        spectra_ref[:, q, :] = stack([turned[:5], turned[64:69]], 1)

    for f in range(2):
        sent = outgoing.at[f, pl.ds(0, 127)]
        pltpu.make_async_copy(sent, sent, out_sems.at[f]).wait()
        for step in range(16):
            forward(f, step).wait_send()
    for slot in range(4):
        pltpu.make_async_copy(coeffs.at[slot], coeffs_hbm.at[slot], coeffs_sems.at[slot]).wait()
    sent = send_a.at[pl.ds(0, 15)]
    pltpu.make_async_copy(sent, sent, fold_send.at[0]).wait()
    sent = send_b.at[pl.ds(0, 31)]
    pltpu.make_async_copy(sent, sent, fold_send.at[1]).wait()


def tiles(wind):
    split = wind.transpose(0, 2, 1, 3).reshape(8, ROWS, 2, COARSE, LANES)
    return split.transpose(0, 1, 3, 2, 4).reshape(80, COARSE, 2, LANES)


def local(wind_u, wind_v, window_m, owner, legendre):
    vmem = pl.BlockSpec(memory_space=pltpu.VMEM)
    hbm = pl.BlockSpec(memory_space=pl.ANY)
    dma = pltpu.SemaphoreType.DMA
    regular = pltpu.SemaphoreType.REGULAR
    coeffs, spectra = pl.pallas_call(
        kernel,
        out_shape=(
            jax.ShapeDtypeStruct((4, 2, 16, 2, COLS), F32),
            jax.ShapeDtypeStruct((5, 2, 16), F32),
        ),
        in_specs=[hbm, hbm, vmem, vmem, hbm],
        out_specs=(hbm, vmem),
        scratch_shapes=[
            pltpu.VMEM((2, COARSE, 80, 2, LANES), BF16),
            pltpu.VMEM((COARSE, ENTRIES), F32),
            pltpu.VMEM((COARSE, ENTRIES), F32),
            pltpu.VMEM((LANES, ENTRIES), F32),
            pltpu.VMEM((LANES, ENTRIES), F32),
            pltpu.VMEM((STEPS, CHUNK * LANES, 2 * ENTRIES), BF16),
            pltpu.VMEM((STEPS, CHUNK * LANES, 2 * ENTRIES), BF16),
            pltpu.VMEM((160, 2 * ENTRIES), F32),
            pltpu.VMEM((4, 192, LANES), F32),
            pltpu.VMEM((2, 128, 5, 2, LANES), BF16),
            pltpu.VMEM((2, 2, 8, 16, 5, 2, LANES), BF16),
            pltpu.VMEM((4, HALF, WIDE), BF16),
            pltpu.VMEM((4, 64, WIDE), F32),
            pltpu.VMEM((4, 2, 16, 2, COLS), F32),
            pltpu.VMEM((64, HALF), F32),
            pltpu.VMEM((16, 8, 3 * LANES), F32),
            pltpu.VMEM((16, 8, 3 * LANES), F32),
            pltpu.VMEM((32, 8, LANES), F32),
            pltpu.VMEM((32, 8, LANES), F32),
            dma((2, STEPS)), dma((4,)), dma((2,)), regular, regular, regular,
            dma((2,)), dma((2, 16)), dma((2, 16)), dma((2, 16)), dma((4,)), dma((2,)), dma((2,)),
        ],
        compiler_params=pltpu.CompilerParams(
            collective_id=0, has_side_effects=True, vmem_limit_bytes=VMEM_BYTES
        ),
    )(tiles(wind_u), tiles(wind_v), window_m[None, :], owner[None, :], legendre)
    return (coeffs, spectra.transpose(1, 2, 0))


def solution(mesh):
    placed = (
        P("deg", None, "wave", None),
        P("deg", None, "wave", None),
        P(),
        P(),
        P("wave", None, "deg"),
    )
    return jax.shard_map(
        local,
        mesh=mesh,
        in_specs=placed,
        out_specs=(P("wave", None, None, None, "deg"), P(None, None, ("wave", "deg"))),
        check_vma=False,
    )
```

```python
import math

import jax
import jax.numpy as jnp
from jax import lax
from jax.experimental import pallas as pl
from jax.experimental.pallas import tpu as pltpu
from jax.sharding import PartitionSpec as P

MESH = pl.DeviceIdType.MESH
BF16 = jnp.bfloat16
F32 = jnp.float32
I32 = jnp.int32
VMEM_BYTES = 56 * 1024 * 1024

NLON = 5120
LANES = 128
COARSE = NLON // LANES
ENTRIES = 256
ROWS = 10
HALF = 1280
COLS = 640
WIDE = COLS + LANES
CHUNK = 4
STEPS = COARSE // CHUNK

NT = (((1,), (1,)), ((), ()))
FAR_PLANES = (4, 3, 5, 2, 6, 1, 7, 0)
FAR_LINES = (2, 1, 3, 0)


def iota(shape, axis):
    return lax.broadcasted_iota(I32, shape, axis)


def one_hot(hits):
    return hits.astype(F32).astype(BF16)


def row_order():
    wanted = iota((320, 320), 0)
    source = wanted % 2 * 160 + wanted // 16 % 2 * 80 + wanted // 2 % 8 * 10 + wanted // 32
    return one_hot(source == iota((320, 320), 1))


def group_order():
    source = iota((160, 160), 1)
    return one_hot(source % 16 * ROWS + source // 16 == iota((160, 160), 0))


def unit_waves(count, window, period):
    phase = iota((count, ENTRIES), 0).astype(F32) * window
    phase = phase - period * jnp.round(phase * (1.0 / period))
    angle = phase * (2.0 * math.pi / period)
    return jnp.cos(angle), jnp.sin(angle)


def stack(pieces, axis):
    return jnp.concatenate(pieces, axis=axis)


def kernel(
    wind_u, wind_v, window_ref, owner_ref, table_hbm, coeffs, spectra_ref,
    winds, coarse_cos, coarse_sin, fine_cos, fine_sin, highs, lows, total, split,
    outgoing, data, table, terms, partial, summed,
    fold_mask, fold_rows, paired_energy, other_energy, fold_out, fold_in, final,
    wind_sems, table_sems, edge_sems,
    out_sems, in_sems, core_send, core_recv, pair_sems, fold_sems, final_sems,
):
    me = lax.axis_index("wave")
    core = lax.axis_index("deg")
    other = 1 - core
    plane = me // 16
    inside = me % 16
    row = inside // 4
    column = inside % 4

    planes = [(plane + away) % 8 * 16 for away in FAR_PLANES]

    def everyone(action):
        def group(index, carry):
            turn_x = index // 4
            turn_y = index % 4
            away_x = 2 + (turn_x + 1) // 2 * (1 - 2 * (turn_x % 2))
            away_y = 2 + (turn_y + 1) // 2 * (1 - 2 * (turn_y % 2))
            base = (row + away_x) % 4 * 4 + (column + away_y) % 4
            for start in planes:
                action(start + base, index)
            return carry

        lax.fori_loop(0, 15, group, 0)
        for start in planes[:7]:
            action(start + inside, 15)

    def wind_copy(f, tile):
        ref = (wind_u, wind_v)[f]
        return pltpu.make_async_copy(ref.at[:, tile], winds.at[f, tile], wind_sems.at[f, tile // CHUNK])

    for tile in range(COARSE):
        wind_copy(0, tile).start()
    barrier = pltpu.get_barrier_semaphore()

    def greet(target, index):
        pl.semaphore_signal(barrier, inc=1, device_id=(target, core), device_id_type=MESH)

    everyone(greet)
    pl.semaphore_signal(barrier, inc=1, device_id=(me, other), device_id_type=MESH)

    def table_copy(slot):
        return pltpu.make_async_copy(
            table_hbm.at[slot], table.at[slot, :, pl.ds(0, COLS)], table_sems.at[slot]
        )

    window = window_ref[...].astype(F32)
    owner = owner_ref[...].astype(F32)
    owner_rows = jnp.broadcast_to(owner, (ENTRIES, ENTRIES))
    same = (jnp.transpose(owner_rows, (1, 0)) == owner_rows) & (
        iota((ENTRIES, ENTRIES), 0) < iota((ENTRIES, ENTRIES), 1)
    )
    rank = jnp.sum(same.astype(F32), axis=0, keepdims=True)
    placing = one_hot(owner_ref[...] == iota((128, ENTRIES), 0))
    rank_masks = [one_hot(rank == float(slot)) for slot in range(4)]

    cos_part, sin_part = unit_waves(COARSE, window, float(COARSE))
    coarse_cos[...] = cos_part
    coarse_sin[...] = sin_part
    cos_part, sin_part = unit_waves(LANES, window, float(NLON))
    fine_cos[...] = cos_part * (1.0 / NLON)
    fine_sin[...] = sin_part * (1.0 / NLON)

    def wind_chunk(f, chunk):
        part = winds.at[f, pl.ds(chunk * CHUNK, CHUNK)]
        pltpu.make_async_copy(part, part, wind_sems.at[f, chunk]).wait()
        return stack(
            [winds.at[f, chunk * CHUNK + inner].reshape(160, LANES)[...] for inner in range(CHUNK)], 1
        )

    def first_step(chunk, carry):
        for inner in range(CHUNK):
            wind_copy(1, chunk * CHUNK + inner).start()
        cos_b = fine_cos[...]
        sin_b = fine_sin[...]
        for inner in range(CHUNK):
            tile = chunk * CHUNK + inner
            cos_a = coarse_cos[pl.ds(tile, 1), :]
            sin_a = coarse_sin[pl.ds(tile, 1), :]
            values = stack([cos_a * cos_b - sin_a * sin_b, -(sin_a * cos_b + cos_a * sin_b)], 1)
            high = values.astype(BF16)
            highs[chunk, LANES * inner : LANES * inner + LANES, :] = high
            lows[chunk, LANES * inner : LANES * inner + LANES, :] = (values - high.astype(F32)).astype(BF16)
        return second_step(0, chunk, carry)

    def second_step(f, chunk, carry):
        part = wind_chunk(f, chunk)
        total[...] += jnp.dot(part, highs[chunk], preferred_element_type=F32) + jnp.dot(
            part, lows[chunk], preferred_element_type=F32
        )
        return carry

    def publish(f):
        for tile in range(4):
            split[tile, :160] = total[:, LANES * tile : LANES * tile + LANES]
        north = stack([split[tile, pl.ds(0, 80, stride=2), :] for tile in range(4)], 1)
        south = stack([split[tile, pl.ds(1, 80, stride=2), :] for tile in range(4)], 1)
        even = (north + south).astype(BF16)
        odd = (north - south).astype(BF16)
        paired = stack([even[:, :ENTRIES], odd[:, :ENTRIES], even[:, ENTRIES:], odd[:, ENTRIES:]], 0)
        ordered = jnp.dot(row_order(), paired, preferred_element_type=F32).astype(BF16)
        blocks = stack(
            [
                ordered[32 * line : 32 * line + 32] * rank_masks[slot]
                for line in range(ROWS)
                for slot in range(4)
            ],
            0,
        )
        placed = lax.dot_general(placing, blocks, NT, preferred_element_type=F32).astype(BF16)
        stacked = stack(
            [
                stack(
                    [placed[16 * g : 16 * g + 16, LANES * line : LANES * line + LANES] for g in range(8)], 1
                )
                for line in range(ROWS)
            ],
            0,
        )
        result = jnp.dot(group_order(), stacked, preferred_element_type=F32).astype(BF16)
        flat = outgoing.at[f].reshape(HALF, LANES)
        for g in range(8):
            flat[160 * g : 160 * g + 160, :] = result[:, LANES * g : LANES * g + LANES]

    def own_copy(f):
        return pltpu.make_async_copy(
            outgoing.at[f, me], data.at[f, core, plane, inside], in_sems.at[f, 15]
        )

    def send_all(f):
        own_copy(f).start()

        def send(target, index):
            pltpu.make_async_remote_copy(
                src_ref=outgoing.at[f, target], dst_ref=data.at[f, core, plane, inside],
                send_sem=out_sems.at[f], recv_sem=in_sems.at[f, index],
                device_id=(target, core), device_id_type=MESH,
            ).start()

        everyone(send)

    def source_of(step):
        return (row + 4 - FAR_LINES[step // 4]) % 4 * 4 + (column + 4 - FAR_LINES[step % 4]) % 4

    def forward(f, step):
        part = data.at[f, core, :, source_of(step)]
        return pltpu.make_async_remote_copy(
            src_ref=part, dst_ref=part, send_sem=core_send.at[f, step], recv_sem=core_recv.at[f, step],
            device_id=(me, other), device_id_type=MESH,
        )

    def forward_all(f):
        for step in range(16):
            part = data.at[f, core, :, source_of(step)]
            pltpu.make_async_copy(part, part, in_sems.at[f, step]).wait()
            forward(f, step).start()
        for step in range(16):
            arrived = data.at[f, other, :, source_of(step)]
            pltpu.make_async_copy(arrived, arrived, core_recv.at[f, step]).wait()

    unit = one_hot(iota((LANES, LANES), 0) == iota((LANES, LANES), 1))

    def project(f):
        turned = [
            lax.dot_general(
                unit, data.at[f, h].reshape(HALF, LANES)[...], NT, preferred_element_type=F32
            ).astype(BF16)
            for h in range(2)
        ]
        results = []
        for slot in range(4):
            if f == 0:
                table_copy(slot).wait()
            rows = stack([turned[h][32 * slot : 32 * slot + 32] for h in range(2)], 0)
            results.append(jnp.dot(rows, table[slot], preferred_element_type=F32))
        return results

    total[...] = jnp.zeros_like(total)
    lax.fori_loop(0, STEPS, first_step, 0)
    publish(0)
    pl.semaphore_wait(barrier, 128)
    send_all(0)
    edge = pltpu.make_async_remote_copy(
        src_ref=table_hbm.at[:, :, pl.ds(pl.multiple_of(other * 512, LANES), LANES)],
        dst_ref=table.at[:, :, pl.ds(COLS, LANES)],
        send_sem=edge_sems.at[0], recv_sem=edge_sems.at[1],
        device_id=(me, other), device_id_type=MESH,
    )
    for slot in range(4):
        table_copy(slot).start()
    edge.start()

    total[...] = jnp.zeros_like(total)
    lax.fori_loop(0, STEPS, lambda chunk, carry: second_step(1, chunk, carry), 0)
    publish(1)
    send_all(1)

    fold_lane = iota((HALF, 2 * LANES), 1)
    fold_turn = fold_lane % 64 // 8
    fold_mask[...] = one_hot(
        (iota((HALF, 2 * LANES), 0) % 10 == fold_lane % LANES // 64 * 5 + fold_turn) & (fold_turn < 5)
    )
    fold_rows[...] = one_hot(iota((LANES, HALF), 1) // 10 == iota((LANES, HALF), 0))
    spread_lane = iota((16, 2 * LANES), 1)
    spread = one_hot(spread_lane // LANES * 8 + spread_lane % 8 == iota((16, 2 * LANES), 0))

    forward_all(0)
    edge.wait()
    first = project(0)

    shape = (32, COLS)
    col = iota(shape, 1)
    even_col = col % 2 == 0
    is_real = iota(shape, 0) % 2 == 0

    def times_unit(values):
        return jnp.where(is_real, -pltpu.roll(values, 31, 0), pltpu.roll(values, 1, 0))

    def neighbours(slot, values):
        wave, last = waves[slot]
        even = stack([values[0:16], values[32:48]], 0)
        odd = stack([values[16:32], values[48:64]], 0)
        flow = jnp.where(even_col, even[:, :COLS], odd[:, :COLS])
        flow = jnp.where(wave + core * COLS + col <= last, flow, 0.0)
        border = jnp.where(core == 0, even[:, COLS : COLS + 1], odd[:, WIDE - 1 :])
        border = jnp.where(wave + COLS - core <= last, border, 0.0)
        before = jnp.where(col == 0, jnp.where(core == 1, border, 0.0), pltpu.roll(flow, 1, 1))
        after = jnp.where(
            col == COLS - 1, jnp.where(core == 0, border, 0.0), pltpu.roll(flow, COLS - 1, 1)
        )
        return before, flow, after

    waves = []
    for slot in range(4):
        hits = ((owner_ref[...] == me) & (rank == float(slot))).astype(F32)
        used = jnp.sum(hits)
        wave = jnp.where(used > 0, jnp.sum(hits * window), float(HALF)).astype(I32)
        waves.append((wave, jnp.where(used > 0, 2 * HALF - 1, -1)))
        degree_row = wave + core * COLS + iota((8, COLS), 1)
        degree = degree_row.astype(F32)
        next_row = degree_row + 1
        squared = wave * wave
        eps_here = jnp.sqrt((degree_row * degree_row - squared).astype(F32) / (4.0 * degree * degree - 1.0))
        eps_next = jnp.sqrt(
            (next_row * next_row - squared).astype(F32) / (4.0 * (degree + 1.0) * (degree + 1.0) - 1.0)
        )
        factor = lax.rsqrt(degree * (degree + 1.0))
        terms[slot, 0] = (degree + 1.0) * eps_here * factor
        terms[slot, 1] = degree * eps_next * factor
        terms[slot, 2] = wave.astype(F32) * factor
        before, flow, after = neighbours(slot, first[slot])
        partial[slot, 0] = terms[slot, 0, :1] * before - terms[slot, 1, :1] * after
        partial[slot, 1] = terms[slot, 2, :1] * times_unit(flow)
    summed[...] = jnp.zeros_like(summed)

    forward_all(1)
    second = project(1)
    for slot in range(4):
        wave, last = waves[slot]
        first_degree = wave + core * COLS
        live = first_degree + col <= last
        before, flow, after = neighbours(slot, second[slot])
        vorticity = partial[slot, 0] + terms[slot, 2, :1] * times_unit(flow)
        divergence = partial[slot, 1] - terms[slot, 0, :1] * before + terms[slot, 1, :1] * after
        vorticity = jnp.where(live, vorticity, 0.0)
        divergence = jnp.where(live, divergence, 0.0)
        coeffs[slot, 0] = vorticity.reshape(16, 2, COLS)
        coeffs[slot, 1] = divergence.reshape(16, 2, COLS)
        vorticity = vorticity * vorticity
        divergence = divergence * divergence
        energy = jnp.where(
            is_real,
            vorticity + pltpu.roll(vorticity, 31, 0),
            divergence + pltpu.roll(divergence, 1, 0),
        )
        wide = stack([energy, jnp.zeros(shape, F32)], 1)
        summed[...] += pltpu.roll(wide, first_degree - HALF, 1)

    for tile in range(HALF // LANES):
        split[tile % 4, 0:32] = summed[:, LANES * tile : LANES * tile + LANES]
        for q in range(2):
            paired_energy[q, :, LANES * tile : LANES * tile + LANES] = split[tile % 4, pl.ds(q, 16, stride=2), :]

    def to_other(src, dst, sems):
        copy = pltpu.make_async_remote_copy(
            src_ref=src, dst_ref=dst, send_sem=sems.at[0], recv_sem=sems.at[1],
            device_id=(me, other), device_id_type=MESH,
        )
        copy.start()
        copy.wait()

    to_other(paired_energy.at[other], other_energy, pair_sems)
    chip_energy = paired_energy[core] + other_energy[...]
    turned = jnp.transpose(chip_energy, (1, 0)).astype(BF16)
    placed = jnp.dot(turned, spread, preferred_element_type=F32).astype(BF16) * fold_mask[...]
    messages = jnp.dot(fold_rows[...], placed, preferred_element_type=F32)
    for half in range(2):
        fold_out[:, half, :] = messages[:, LANES * half : LANES * half + LANES]
    fold_in[me] = fold_out[me]

    def send_fold(target, index):
        pltpu.make_async_remote_copy(
            src_ref=fold_out.at[target], dst_ref=fold_in.at[me],
            send_sem=fold_sems.at[0], recv_sem=fold_sems.at[1],
            device_id=(target, core), device_id_type=MESH,
        ).start()

    everyone(send_fold)
    arrived = fold_in.at[pl.ds(0, 127)]
    pltpu.make_async_copy(arrived, arrived, fold_sems.at[1]).wait()
    lines = fold_in.reshape(2 * LANES, LANES)
    folded = lines[0:8, :]
    for index in range(1, 32):
        folded = folded + lines[8 * index : 8 * index + 8, :]
    final[core] = folded[0:2] + folded[2:4] + folded[4:6] + folded[6:8]
    to_other(final.at[core], final.at[core], final_sems)
    halves = []
    for half in range(2):
        values = final[:, half, :] * (1.0 / ENTRIES)
        halves.append(jnp.where(core == 1, pltpu.roll(values, 64, 1), values))
    for index in range(5):
        spectra_ref[index] = stack([values[:, 8 * index : 8 * index + 8] for values in halves], 1)

    for f in range(2):
        sent = outgoing.at[f, pl.ds(0, 127)]
        pltpu.make_async_copy(sent, sent, out_sems.at[f]).wait()
        for step in range(16):
            forward(f, step).wait_send()
    sent = fold_out.at[pl.ds(0, 127)]
    pltpu.make_async_copy(sent, sent, fold_sems.at[0]).wait()


def tiles(wind):
    split = wind.transpose(0, 2, 1, 3).reshape(8, ROWS, 2, COARSE, LANES)
    return split.transpose(0, 1, 3, 2, 4).reshape(80, COARSE, 2, LANES)


def local(wind_u, wind_v, window_m, owner, legendre):
    vmem = pl.BlockSpec(memory_space=pltpu.VMEM)
    hbm = pl.BlockSpec(memory_space=pl.ANY)
    dma = pltpu.SemaphoreType.DMA
    coeffs, spectra = pl.pallas_call(
        kernel,
        out_shape=(pltpu.VMEM((4, 2, 16, 2, COLS), F32), pltpu.VMEM((5, 2, 16), F32)),
        in_specs=[hbm, hbm, vmem, vmem, hbm],
        out_specs=(vmem, vmem),
        scratch_shapes=[
            pltpu.VMEM((2, COARSE, 80, 2, LANES), BF16),
            pltpu.VMEM((COARSE, ENTRIES), F32),
            pltpu.VMEM((COARSE, ENTRIES), F32),
            pltpu.VMEM((LANES, ENTRIES), F32),
            pltpu.VMEM((LANES, ENTRIES), F32),
            pltpu.VMEM((STEPS, CHUNK * LANES, 2 * ENTRIES), BF16),
            pltpu.VMEM((STEPS, CHUNK * LANES, 2 * ENTRIES), BF16),
            pltpu.VMEM((160, 2 * ENTRIES), F32),
            pltpu.VMEM((4, 192, LANES), F32),
            pltpu.VMEM((2, 128, 5, 2, LANES), BF16),
            pltpu.VMEM((2, 2, 8, 16, 5, 2, LANES), BF16),
            pltpu.VMEM((4, HALF, WIDE), BF16),
            pltpu.VMEM((4, 3, 8, COLS), F32),
            pltpu.VMEM((4, 2, 32, COLS), F32),
            pltpu.VMEM((32, HALF), F32),
            pltpu.VMEM((HALF, 2 * LANES), BF16),
            pltpu.VMEM((LANES, HALF), BF16),
            pltpu.VMEM((2, 16, HALF), F32),
            pltpu.VMEM((16, HALF), F32),
            pltpu.VMEM((LANES, 2, LANES), F32),
            pltpu.VMEM((LANES, 2, LANES), F32),
            pltpu.VMEM((2, 2, LANES), F32),
            dma((2, STEPS)), dma((4,)), dma((2,)),
            dma((2,)), dma((2, 16)), dma((2, 16)), dma((2, 16)),
            dma((2,)), dma((2,)), dma((2,)),
        ],
        compiler_params=pltpu.CompilerParams(
            collective_id=0, has_side_effects=True, vmem_limit_bytes=VMEM_BYTES
        ),
    )(tiles(wind_u), tiles(wind_v), window_m[None, :], owner[None, :], legendre)
    return (coeffs, spectra.transpose(1, 2, 0))


def solution(mesh):
    placed = (
        P("deg", None, "wave", None),
        P("deg", None, "wave", None),
        P(),
        P(),
        P("wave", None, "deg"),
    )
    return jax.shard_map(
        local,
        mesh=mesh,
        in_specs=placed,
        out_specs=(P("wave", None, None, None, "deg"), P(None, None, ("wave", "deg"))),
        check_vma=False,
    )
```

```python
import math

import jax
import jax.numpy as jnp
from jax import lax
from jax.experimental import pallas as pl
from jax.experimental.pallas import tpu as pltpu
from jax.sharding import PartitionSpec as P

MESH = pl.DeviceIdType.MESH
BF16 = jnp.bfloat16
F32 = jnp.float32
I32 = jnp.int32
VMEM_BYTES = 56 * 1024 * 1024

NLON = 5120
LANES = 128
COARSE = NLON // LANES
ENTRIES = 256
ROWS = 10
HALF = 1280
COLS = 640
WIDE = COLS + LANES
CHUNK = 20
STEPS = COARSE // CHUNK

NT = (((1,), (1,)), ((), ()))
FAR_PLANES = (4, 3, 5, 2, 6, 1, 7, 0)
FAR_LINES = (2, 1, 3, 0)


def iota(shape, axis):
    return lax.broadcasted_iota(I32, shape, axis)


def one_hot(hits):
    return hits.astype(F32).astype(BF16)


def row_order():
    wanted = iota((320, 320), 0)
    source = wanted % 2 * 160 + wanted // 16 % 2 * 80 + wanted // 2 % 8 * 10 + wanted // 32
    return one_hot(source == iota((320, 320), 1))


def group_order():
    source = iota((160, 160), 1)
    return one_hot(source % 16 * ROWS + source // 16 == iota((160, 160), 0))


def unit_waves(count, window, period):
    phase = iota((count, ENTRIES), 0).astype(F32) * window
    phase = phase - period * jnp.round(phase * (1.0 / period))
    angle = phase * (2.0 * math.pi / period)
    return jnp.cos(angle), jnp.sin(angle)


def stack(pieces, axis):
    return jnp.concatenate(pieces, axis=axis)


def kernel(
    wind_u, wind_v, window_ref, owner_ref, table_hbm, coeffs, spectra_ref,
    winds, coarse_cos, coarse_sin, fine_cos, fine_sin, waves_table, total, split,
    outgoing, data, table, terms, partial, summed,
    fold_mask, fold_rows, paired_energy, other_energy, fold_out, fold_in, final,
    wind_sems, table_sems, edge_sems,
    out_sems, in_sems, core_send, core_recv, pair_sems, fold_sems, final_sems,
):
    me = lax.axis_index("wave")
    core = lax.axis_index("deg")
    other = 1 - core
    plane = me // 16
    inside = me % 16
    row = inside // 4
    column = inside % 4

    planes = [(plane + away) % 8 * 16 for away in FAR_PLANES]

    def group_base(index):
        turn_x = index // 4
        turn_y = index % 4
        away_x = 2 + (turn_x + 1) // 2 * (1 - 2 * (turn_x % 2))
        away_y = 2 + (turn_y + 1) // 2 * (1 - 2 * (turn_y % 2))
        return (row + away_x) % 4 * 4 + (column + away_y) % 4

    def everyone(action):
        def group(index, carry):
            base = group_base(index)
            for start in planes:
                action(start + base, index)
            return carry

        lax.fori_loop(0, 15, group, 0)
        for start in planes[:7]:
            action(start + inside, 15)

    def wind_copy(f, tile):
        ref = (wind_u, wind_v)[f]
        return pltpu.make_async_copy(ref.at[:, tile], winds.at[f, tile], wind_sems.at[f, tile // CHUNK])

    for tile in range(COARSE):
        wind_copy(0, tile).start()
    barrier = pltpu.get_barrier_semaphore()

    def greet_group(index, carry):
        base = group_base(index)
        for start in planes[:7]:
            pl.semaphore_signal(barrier, inc=1, device_id=(start + base, core), device_id_type=MESH)
        side = jnp.where(base == inside, other, core)
        pl.semaphore_signal(barrier, inc=1, device_id=(planes[7] + base, side), device_id_type=MESH)
        return carry

    lax.fori_loop(0, 16, greet_group, 0)

    def table_copy(slot):
        return pltpu.make_async_copy(
            table_hbm.at[slot], table.at[slot, :, pl.ds(0, COLS)], table_sems.at[slot]
        )

    window = window_ref[...].astype(F32)
    owner = owner_ref[...].astype(F32)
    owner_rows = jnp.broadcast_to(owner, (ENTRIES, ENTRIES))
    same = (jnp.transpose(owner_rows, (1, 0)) == owner_rows) & (
        iota((ENTRIES, ENTRIES), 0) < iota((ENTRIES, ENTRIES), 1)
    )
    rank = jnp.sum(same.astype(F32), axis=0, keepdims=True)
    placing = one_hot(owner_ref[...] == iota((128, ENTRIES), 0))
    rank_masks = [one_hot(rank == float(slot)) for slot in range(4)]

    cos_part, sin_part = unit_waves(COARSE, window, float(COARSE))
    coarse_cos[...] = cos_part
    coarse_sin[...] = sin_part
    cos_part, sin_part = unit_waves(LANES, window, float(NLON))
    fine_cos[...] = cos_part * (1.0 / NLON)
    fine_sin[...] = sin_part * (1.0 / NLON)

    def wind_chunk(f, chunk):
        part = winds.at[f, pl.ds(chunk * CHUNK, CHUNK)]
        pltpu.make_async_copy(part, part, wind_sems.at[f, chunk]).wait()
        return stack(
            [winds.at[f, chunk * CHUNK + inner].reshape(160, LANES)[...] for inner in range(CHUNK)], 1
        )

    def prepare(step, carry):
        cos_b = fine_cos[...]
        sin_b = fine_sin[...]
        for inner in range(5):
            tile = step * 5 + inner
            wind_copy(1, tile).start()
            cos_a = coarse_cos[pl.ds(tile, 1), :]
            sin_a = coarse_sin[pl.ds(tile, 1), :]
            values = stack([cos_a * cos_b - sin_a * sin_b, -(sin_a * cos_b + cos_a * sin_b)], 1)
            high = values.astype(BF16)
            first = (tile // CHUNK * CHUNK + tile) * LANES
            waves_table[pl.ds(pl.multiple_of(first, LANES), LANES), :] = high
            second = first + CHUNK * LANES
            low = (values - high.astype(F32)).astype(BF16)
            waves_table[pl.ds(pl.multiple_of(second, LANES), LANES), :] = low
        return carry

    def transform(f):
        def step(chunk, carry):
            part = wind_chunk(f, chunk)
            depth = 2 * CHUNK * LANES
            here = pl.ds(pl.multiple_of(chunk * depth, depth), depth)
            total[...] += jnp.dot(
                stack([part, part], 1), waves_table[here, :], preferred_element_type=F32
            )
            return carry

        total[...] = jnp.zeros_like(total)
        lax.fori_loop(0, STEPS, step, 0)

    def publish(f):
        for tile in range(4):
            split[tile, :160] = total[:, LANES * tile : LANES * tile + LANES]
        north = stack([split[tile, pl.ds(0, 80, stride=2), :] for tile in range(4)], 1)
        south = stack([split[tile, pl.ds(1, 80, stride=2), :] for tile in range(4)], 1)
        even = (north + south).astype(BF16)
        odd = (north - south).astype(BF16)
        paired = stack([even[:, :ENTRIES], odd[:, :ENTRIES], even[:, ENTRIES:], odd[:, ENTRIES:]], 0)
        ordered = jnp.dot(row_order(), paired, preferred_element_type=F32).astype(BF16)
        blocks = stack(
            [
                ordered[32 * line : 32 * line + 32] * rank_masks[slot]
                for line in range(ROWS)
                for slot in range(4)
            ],
            0,
        )
        placed = lax.dot_general(placing, blocks, NT, preferred_element_type=F32).astype(BF16)
        stacked = stack(
            [
                stack(
                    [placed[16 * g : 16 * g + 16, LANES * line : LANES * line + LANES] for g in range(8)], 1
                )
                for line in range(ROWS)
            ],
            0,
        )
        result = jnp.dot(group_order(), stacked, preferred_element_type=F32).astype(BF16)
        flat = outgoing.at[f].reshape(HALF, LANES)
        for g in range(8):
            flat[160 * g : 160 * g + 160, :] = result[:, LANES * g : LANES * g + LANES]

    def own_copy(f):
        return pltpu.make_async_copy(
            outgoing.at[f, me], data.at[f, core, plane, inside], in_sems.at[f, 15]
        )

    def send_all(f):
        own_copy(f).start()

        def send(target, index):
            pltpu.make_async_remote_copy(
                src_ref=outgoing.at[f, target], dst_ref=data.at[f, core, plane, inside],
                send_sem=out_sems.at[f], recv_sem=in_sems.at[f, index],
                device_id=(target, core), device_id_type=MESH,
            ).start()

        everyone(send)

    def source_of(step):
        return (row + 4 - FAR_LINES[step // 4]) % 4 * 4 + (column + 4 - FAR_LINES[step % 4]) % 4

    def forward(f, step):
        part = data.at[f, core, :, source_of(step)]
        return pltpu.make_async_remote_copy(
            src_ref=part, dst_ref=part, send_sem=core_send.at[f, step], recv_sem=core_recv.at[f, step],
            device_id=(me, other), device_id_type=MESH,
        )

    def forward_start(f, steps):
        for step in steps:
            part = data.at[f, core, :, source_of(step)]
            pltpu.make_async_copy(part, part, in_sems.at[f, step]).wait()
            forward(f, step).start()

    def forward_wait(f):
        for step in range(16):
            arrived = data.at[f, other, :, source_of(step)]
            pltpu.make_async_copy(arrived, arrived, core_recv.at[f, step]).wait()

    unit = one_hot(iota((LANES, LANES), 0) == iota((LANES, LANES), 1))

    def turn(f):
        return [
            lax.dot_general(
                unit, data.at[f, h].reshape(HALF, LANES)[...], NT, preferred_element_type=F32
            ).astype(BF16)
            for h in range(2)
        ]

    def project(turned, slot):
        rows = stack([turned[h][32 * slot : 32 * slot + 32] for h in range(2)], 0)
        return jnp.dot(rows, table[slot], preferred_element_type=F32)

    lax.fori_loop(0, 8, prepare, 0)
    transform(0)
    publish(0)
    pl.semaphore_wait(barrier, 128)
    send_all(0)
    edge = pltpu.make_async_remote_copy(
        src_ref=table_hbm.at[:, :, pl.ds(pl.multiple_of(other * 512, LANES), LANES)],
        dst_ref=table.at[:, :, pl.ds(COLS, LANES)],
        send_sem=edge_sems.at[0], recv_sem=edge_sems.at[1],
        device_id=(me, other), device_id_type=MESH,
    )
    for slot in range(4):
        table_copy(slot).start()
    edge.start()

    transform(1)
    publish(1)
    send_all(1)

    fold_lane = iota((HALF, 2 * LANES), 1)
    fold_turn = fold_lane % 64 // 8
    fold_mask[...] = one_hot(
        (iota((HALF, 2 * LANES), 0) % 10 == fold_lane % LANES // 64 * 5 + fold_turn) & (fold_turn < 5)
    )
    fold_rows[...] = one_hot(iota((LANES, HALF), 1) // 10 == iota((LANES, HALF), 0))
    spread_lane = iota((16, 2 * LANES), 1)
    spread = one_hot(spread_lane // LANES * 8 + spread_lane % 8 == iota((16, 2 * LANES), 0))

    forward_start(0, range(16))
    forward_wait(0)
    edge.wait()
    for slot in range(4):
        table_copy(slot).wait()
    turned = turn(0)

    shape = (32, COLS)
    col = iota(shape, 1)
    even_col = col % 2 == 0
    is_real = iota(shape, 0) % 2 == 0

    def times_unit(values):
        return jnp.where(is_real, -pltpu.roll(values, 31, 0), pltpu.roll(values, 1, 0))

    def neighbours(slot, values):
        wave, last = waves[slot]
        even = stack([values[0:16], values[32:48]], 0)
        odd = stack([values[16:32], values[48:64]], 0)
        flow = jnp.where(even_col, even[:, :COLS], odd[:, :COLS])
        flow = jnp.where(wave + core * COLS + col <= last, flow, 0.0)
        border = jnp.where(core == 0, even[:, COLS : COLS + 1], odd[:, WIDE - 1 :])
        border = jnp.where(wave + COLS - core <= last, border, 0.0)
        before = jnp.where(col == 0, jnp.where(core == 1, border, 0.0), pltpu.roll(flow, 1, 1))
        after = jnp.where(
            col == COLS - 1, jnp.where(core == 0, border, 0.0), pltpu.roll(flow, COLS - 1, 1)
        )
        return before, flow, after

    waves = []
    ready = (range(0, 5), range(5, 9), range(9, 12), range(12, 13))
    for slot in range(4):
        forward_start(1, ready[slot])
        hits = ((owner_ref[...] == me) & (rank == float(slot))).astype(F32)
        used = jnp.sum(hits)
        wave = jnp.where(used > 0, jnp.sum(hits * window), float(HALF)).astype(I32)
        waves.append((wave, jnp.where(used > 0, 2 * HALF - 1, -1)))
        degree_row = wave + core * COLS + iota((8, COLS), 1)
        degree = degree_row.astype(F32)
        next_row = degree_row + 1
        squared = wave * wave
        eps_here = jnp.sqrt((degree_row * degree_row - squared).astype(F32) / (4.0 * degree * degree - 1.0))
        eps_next = jnp.sqrt(
            (next_row * next_row - squared).astype(F32) / (4.0 * (degree + 1.0) * (degree + 1.0) - 1.0)
        )
        factor = lax.rsqrt(degree * (degree + 1.0))
        terms[slot, 0] = (degree + 1.0) * eps_here * factor
        terms[slot, 1] = degree * eps_next * factor
        terms[slot, 2] = wave.astype(F32) * factor
        before, flow, after = neighbours(slot, project(turned, slot))
        partial[slot, 0] = terms[slot, 0, :1] * before - terms[slot, 1, :1] * after
        partial[slot, 1] = terms[slot, 2, :1] * times_unit(flow)
    summed[...] = jnp.zeros_like(summed)

    forward_start(1, range(13, 16))
    forward_wait(1)
    turned = turn(1)
    for slot in range(4):
        wave, last = waves[slot]
        first_degree = wave + core * COLS
        live = first_degree + col <= last
        before, flow, after = neighbours(slot, project(turned, slot))
        vorticity = partial[slot, 0] + terms[slot, 2, :1] * times_unit(flow)
        divergence = partial[slot, 1] - terms[slot, 0, :1] * before + terms[slot, 1, :1] * after
        vorticity = jnp.where(live, vorticity, 0.0)
        divergence = jnp.where(live, divergence, 0.0)
        coeffs[slot, 0] = vorticity.reshape(16, 2, COLS)
        coeffs[slot, 1] = divergence.reshape(16, 2, COLS)
        vorticity = vorticity * vorticity
        divergence = divergence * divergence
        energy = jnp.where(
            is_real,
            vorticity + pltpu.roll(vorticity, 31, 0),
            divergence + pltpu.roll(divergence, 1, 0),
        )
        wide = stack([energy, jnp.zeros(shape, F32)], 1)
        summed[...] += pltpu.roll(wide, first_degree - HALF, 1)

    for tile in range(HALF // LANES):
        split[tile % 4, 0:32] = summed[:, LANES * tile : LANES * tile + LANES]
        for q in range(2):
            paired_energy[q, :, LANES * tile : LANES * tile + LANES] = split[tile % 4, pl.ds(q, 16, stride=2), :]

    def to_other(src, dst, sems):
        copy = pltpu.make_async_remote_copy(
            src_ref=src, dst_ref=dst, send_sem=sems.at[0], recv_sem=sems.at[1],
            device_id=(me, other), device_id_type=MESH,
        )
        copy.start()
        copy.wait()

    to_other(paired_energy.at[other], other_energy, pair_sems)
    chip_energy = paired_energy[core] + other_energy[...]
    upright = jnp.transpose(chip_energy, (1, 0)).astype(BF16)
    placed = jnp.dot(upright, spread, preferred_element_type=F32).astype(BF16) * fold_mask[...]
    messages = jnp.dot(fold_rows[...], placed, preferred_element_type=F32)
    for half in range(2):
        fold_out[:, half, :] = messages[:, LANES * half : LANES * half + LANES]
    fold_in[me] = fold_out[me]

    def send_fold(target, index):
        pltpu.make_async_remote_copy(
            src_ref=fold_out.at[target], dst_ref=fold_in.at[me],
            send_sem=fold_sems.at[0], recv_sem=fold_sems.at[1],
            device_id=(target, core), device_id_type=MESH,
        ).start()

    everyone(send_fold)
    arrived = fold_in.at[pl.ds(0, 127)]
    pltpu.make_async_copy(arrived, arrived, fold_sems.at[1]).wait()
    lines = fold_in.reshape(2 * LANES, LANES)
    folded = lines[0:8, :]
    for index in range(1, 32):
        folded = folded + lines[8 * index : 8 * index + 8, :]
    final[core] = folded[0:2] + folded[2:4] + folded[4:6] + folded[6:8]
    to_other(final.at[core], final.at[core], final_sems)
    halves = []
    for half in range(2):
        values = final[:, half, :] * (1.0 / ENTRIES)
        halves.append(jnp.where(core == 1, pltpu.roll(values, 64, 1), values))
    for index in range(5):
        spectra_ref[index] = stack([values[:, 8 * index : 8 * index + 8] for values in halves], 1)

    for f in range(2):
        sent = outgoing.at[f, pl.ds(0, 127)]
        pltpu.make_async_copy(sent, sent, out_sems.at[f]).wait()
        for step in range(16):
            forward(f, step).wait_send()
    sent = fold_out.at[pl.ds(0, 127)]
    pltpu.make_async_copy(sent, sent, fold_sems.at[0]).wait()


def tiles(wind):
    split = wind.transpose(0, 2, 1, 3).reshape(8, ROWS, 2, COARSE, LANES)
    return split.transpose(0, 1, 3, 2, 4).reshape(80, COARSE, 2, LANES)


def local(wind_u, wind_v, window_m, owner, legendre):
    vmem = pl.BlockSpec(memory_space=pltpu.VMEM)
    hbm = pl.BlockSpec(memory_space=pl.ANY)
    dma = pltpu.SemaphoreType.DMA
    coeffs, spectra = pl.pallas_call(
        kernel,
        out_shape=(pltpu.VMEM((4, 2, 16, 2, COLS), F32), pltpu.VMEM((5, 2, 16), F32)),
        in_specs=[hbm, hbm, vmem, vmem, hbm],
        out_specs=(vmem, vmem),
        scratch_shapes=[
            pltpu.VMEM((2, COARSE, 80, 2, LANES), BF16),
            pltpu.VMEM((COARSE, ENTRIES), F32),
            pltpu.VMEM((COARSE, ENTRIES), F32),
            pltpu.VMEM((LANES, ENTRIES), F32),
            pltpu.VMEM((LANES, ENTRIES), F32),
            pltpu.VMEM((2 * NLON, 2 * ENTRIES), BF16),
            pltpu.VMEM((160, 2 * ENTRIES), F32),
            pltpu.VMEM((4, 192, LANES), F32),
            pltpu.VMEM((2, 128, 5, 2, LANES), BF16),
            pltpu.VMEM((2, 2, 8, 16, 5, 2, LANES), BF16),
            pltpu.VMEM((4, HALF, WIDE), BF16),
            pltpu.VMEM((4, 3, 8, COLS), F32),
            pltpu.VMEM((4, 2, 32, COLS), F32),
            pltpu.VMEM((32, HALF), F32),
            pltpu.VMEM((HALF, 2 * LANES), BF16),
            pltpu.VMEM((LANES, HALF), BF16),
            pltpu.VMEM((2, 16, HALF), F32),
            pltpu.VMEM((16, HALF), F32),
            pltpu.VMEM((LANES, 2, LANES), F32),
            pltpu.VMEM((LANES, 2, LANES), F32),
            pltpu.VMEM((2, 2, LANES), F32),
            dma((2, STEPS)), dma((4,)), dma((2,)),
            dma((2,)), dma((2, 16)), dma((2, 16)), dma((2, 16)),
            dma((2,)), dma((2,)), dma((2,)),
        ],
        compiler_params=pltpu.CompilerParams(
            collective_id=0, has_side_effects=True, vmem_limit_bytes=VMEM_BYTES
        ),
    )(tiles(wind_u), tiles(wind_v), window_m[None, :], owner[None, :], legendre)
    return (coeffs, spectra.transpose(1, 2, 0))


def solution(mesh):
    placed = (
        P("deg", None, "wave", None),
        P("deg", None, "wave", None),
        P(),
        P(),
        P("wave", None, "deg"),
    )
    return jax.shard_map(
        local,
        mesh=mesh,
        in_specs=placed,
        out_specs=(P("wave", None, None, None, "deg"), P(None, None, ("wave", "deg"))),
        check_vma=False,
    )
```

```python
import math

import jax
import jax.numpy as jnp
from jax import lax
from jax.experimental import pallas as pl
from jax.experimental.pallas import tpu as pltpu
from jax.sharding import PartitionSpec as P

MESH = pl.DeviceIdType.MESH
BF16 = jnp.bfloat16
F32 = jnp.float32
I32 = jnp.int32
VMEM_BYTES = 56 * 1024 * 1024

NLON = 5120
LANES = 128
COARSE = NLON // LANES
ENTRIES = 256
ROWS = 10
HALF = 1280
COLS = 640
CHUNK = 20
STEPS = COARSE // CHUNK

NT = (((1,), (1,)), ((), ()))
FAR_PLANES = (4, 3, 5, 2, 6, 1, 7, 0)
FAR_LINES = (2, 1, 3, 0)


def iota(shape, axis):
    return lax.broadcasted_iota(I32, shape, axis)


def one_hot(hits):
    return hits.astype(F32).astype(BF16)


def row_order():
    wanted = iota((320, 320), 0)
    source = wanted % 2 * 160 + wanted // 16 % 2 * 80 + wanted // 2 % 8 * 10 + wanted // 32
    return one_hot(source == iota((320, 320), 1))


def group_order():
    source = iota((160, 160), 1)
    return one_hot(source % 16 * ROWS + source // 16 == iota((160, 160), 0))


def unit_waves(count, window, period):
    phase = iota((count, ENTRIES), 0).astype(F32) * window
    phase = phase - period * jnp.round(phase * (1.0 / period))
    angle = phase * (2.0 * math.pi / period)
    return jnp.cos(angle), jnp.sin(angle)


def stack(pieces, axis):
    return jnp.concatenate(pieces, axis=axis)


def kernel(
    wind_u, wind_v, window_ref, owner_ref, table_hbm, coeffs, spectra_ref,
    winds, coarse_cos, coarse_sin, fine_cos, fine_sin, waves_table, total, split,
    outgoing, data, table, terms, partial, summed, coeffs_out,
    fold_mask, fold_rows, fold_out, fold_in, final,
    wind_sems, table_sems, share_send, share_recv, meet,
    out_sems, in_sems, coeffs_send, coeffs_recv, fold_sems, final_sems,
):
    me = lax.axis_index("wave")
    core = lax.axis_index("deg")
    other = 1 - core
    plane = me // 16
    inside = me % 16
    row = inside // 4
    column = inside % 4

    planes = [(plane + away) % 8 * 16 for away in FAR_PLANES]

    def group_base(index):
        turn_x = index // 4
        turn_y = index % 4
        away_x = 2 + (turn_x + 1) // 2 * (1 - 2 * (turn_x % 2))
        away_y = 2 + (turn_y + 1) // 2 * (1 - 2 * (turn_y % 2))
        return (row + away_x) % 4 * 4 + (column + away_y) % 4

    def everyone(action):
        def group(index, carry):
            base = group_base(index)
            for start in planes:
                action(start + base, index)
            return carry

        lax.fori_loop(0, 15, group, 0)
        for start in planes[:7]:
            action(start + inside, 15)

    def wind_copy(f, tile):
        ref = (wind_u, wind_v)[f]
        return pltpu.make_async_copy(ref.at[:, tile], winds.at[f, tile], wind_sems.at[f, tile // CHUNK])

    for tile in range(COARSE):
        wind_copy(0, tile).start()
    def greet_plane(sem):
        def greet(step, carry):
            there = plane * 16 + (inside + step) % 16
            pl.semaphore_signal(sem, inc=1, device_id=(there, core), device_id_type=MESH)
            return carry

        lax.fori_loop(1, 16, greet, 0)

    def greet_line(step, carry):
        there = (plane + step) % 8 * 16 + inside
        pl.semaphore_signal(barrier, inc=1, device_id=(there, core), device_id_type=MESH)
        return carry

    barrier = pltpu.get_barrier_semaphore()
    pl.semaphore_signal(barrier, inc=1, device_id=(me, other), device_id_type=MESH)
    lax.fori_loop(1, 8, greet_line, 0)
    greet_plane(barrier)

    own_half = pl.ds(pl.multiple_of(core * COLS, LANES), COLS)

    def table_copy(slot):
        return pltpu.make_async_copy(table_hbm.at[slot], table.at[slot, :, own_half], table_sems.at[slot])

    def table_share(slot):
        return pltpu.make_async_remote_copy(
            src_ref=table_hbm.at[slot], dst_ref=table.at[slot, :, own_half],
            send_sem=share_send.at[slot], recv_sem=share_recv.at[slot],
            device_id=(me, other), device_id_type=MESH,
        )

    def table_ready(slot):
        table_copy(slot).wait()
        half = table.at[slot, :, pl.ds(pl.multiple_of(other * COLS, LANES), COLS)]
        pltpu.make_async_copy(half, half, share_recv.at[slot]).wait()

    window = window_ref[...].astype(F32)
    owner = owner_ref[...].astype(F32)
    owner_rows = jnp.broadcast_to(owner, (ENTRIES, ENTRIES))
    same = (jnp.transpose(owner_rows, (1, 0)) == owner_rows) & (
        iota((ENTRIES, ENTRIES), 0) < iota((ENTRIES, ENTRIES), 1)
    )
    rank = jnp.sum(same.astype(F32), axis=0, keepdims=True)
    placing = one_hot(owner_ref[...] == iota((128, ENTRIES), 0))
    rank_masks = [one_hot(rank == float(slot)) for slot in range(4)]

    cos_part, sin_part = unit_waves(COARSE, window, float(COARSE))
    coarse_cos[...] = cos_part
    coarse_sin[...] = sin_part
    cos_part, sin_part = unit_waves(LANES, window, float(NLON))
    fine_cos[...] = cos_part * (1.0 / NLON)
    fine_sin[...] = sin_part * (1.0 / NLON)

    def wind_chunk(f, chunk):
        part = winds.at[f, pl.ds(chunk * CHUNK, CHUNK)]
        pltpu.make_async_copy(part, part, wind_sems.at[f, chunk]).wait()
        return stack(
            [winds.at[f, chunk * CHUNK + inner].reshape(160, LANES)[...] for inner in range(CHUNK)], 1
        )

    def prepare(step, carry):
        cos_b = fine_cos[...]
        sin_b = fine_sin[...]
        for inner in range(5):
            tile = step * 5 + inner
            wind_copy(1, tile).start()
            cos_a = coarse_cos[pl.ds(tile, 1), :]
            sin_a = coarse_sin[pl.ds(tile, 1), :]
            values = stack([cos_a * cos_b - sin_a * sin_b, -(sin_a * cos_b + cos_a * sin_b)], 1)
            high = values.astype(BF16)
            first = (tile // CHUNK * CHUNK + tile) * LANES
            waves_table[pl.ds(pl.multiple_of(first, LANES), LANES), :] = high
            second = first + CHUNK * LANES
            low = (values - high.astype(F32)).astype(BF16)
            waves_table[pl.ds(pl.multiple_of(second, LANES), LANES), :] = low
        return carry

    def transform(f):
        def step(chunk, carry):
            part = wind_chunk(f, chunk)
            depth = 2 * CHUNK * LANES
            here = pl.ds(pl.multiple_of(chunk * depth, depth), depth)
            total[...] += jnp.dot(
                stack([part, part], 1), waves_table[here, :], preferred_element_type=F32
            )
            return carry

        total[...] = jnp.zeros_like(total)
        lax.fori_loop(0, STEPS, step, 0)

    def publish(f):
        for tile in range(4):
            split[tile, :160] = total[:, LANES * tile : LANES * tile + LANES]
        north = stack([split[tile, pl.ds(0, 80, stride=2), :] for tile in range(4)], 1)
        south = stack([split[tile, pl.ds(1, 80, stride=2), :] for tile in range(4)], 1)
        even = (north + south).astype(BF16)
        odd = (north - south).astype(BF16)
        paired = stack([even[:, :ENTRIES], odd[:, :ENTRIES], even[:, ENTRIES:], odd[:, ENTRIES:]], 0)
        ordered = jnp.dot(row_order(), paired, preferred_element_type=F32).astype(BF16)
        blocks = stack(
            [
                ordered[32 * line : 32 * line + 32] * rank_masks[slot]
                for line in range(ROWS)
                for slot in range(4)
            ],
            0,
        )
        placed = lax.dot_general(placing, blocks, NT, preferred_element_type=F32).astype(BF16)
        stacked = stack(
            [
                stack(
                    [placed[16 * g : 16 * g + 16, LANES * line : LANES * line + LANES] for g in range(8)], 1
                )
                for line in range(ROWS)
            ],
            0,
        )
        result = jnp.dot(group_order(), stacked, preferred_element_type=F32).astype(BF16)
        flat = outgoing.at[f].reshape(HALF, LANES)
        for g in range(8):
            flat[160 * g : 160 * g + 160, :] = result[:, LANES * g : LANES * g + LANES]

    def own_copy(f):
        return pltpu.make_async_copy(
            outgoing.at[f, me], data.at[f, plane, inside], in_sems.at[f, 15]
        )

    def send_all(f):
        own_copy(f).start()

        def send(target, index):
            pltpu.make_async_remote_copy(
                src_ref=outgoing.at[f, target], dst_ref=data.at[f, plane, inside],
                send_sem=out_sems.at[f], recv_sem=in_sems.at[f, index],
                device_id=(target, core), device_id_type=MESH,
            ).start()

        everyone(send)

    def arrive(f):
        for step in range(16):
            source = (row + 4 - FAR_LINES[step // 4]) % 4 * 4 + (column + 4 - FAR_LINES[step % 4]) % 4
            part = data.at[f, :, source]
            pltpu.make_async_copy(part, part, in_sems.at[f, step]).wait()

    unit = one_hot(iota((LANES, LANES), 0) == iota((LANES, LANES), 1))

    def turn(f):
        return lax.dot_general(
            unit, data.at[f].reshape(HALF, LANES)[...], NT, preferred_element_type=F32
        ).astype(BF16)

    def project(turned, slot):
        return jnp.dot(turned[32 * slot : 32 * slot + 32], table[slot], preferred_element_type=F32)

    lax.fori_loop(0, 8, prepare, 0)
    pl.semaphore_wait(barrier, 23)
    greet_plane(meet)
    transform(0)
    publish(0)
    pl.semaphore_wait(meet, 15)
    send_all(0)
    for slot in range(4):
        table_copy(slot).start()

    transform(1)
    publish(1)
    send_all(1)
    for slot in range(4):
        table_share(slot).start()

    fold_lane = iota((HALF, 2 * LANES), 1)
    fold_turn = fold_lane % 64 // 8
    fold_mask[...] = one_hot(
        (iota((HALF, 2 * LANES), 0) % 10 == fold_lane % LANES // 64 * 5 + fold_turn) & (fold_turn < 5)
    )
    fold_rows[...] = one_hot(iota((LANES, HALF), 1) // 10 == iota((LANES, HALF), 0))
    spread_row = iota((16, 2 * LANES), 0)
    spread_lane = iota((16, 2 * LANES), 1)
    spread = one_hot((spread_row % 2 == spread_lane // LANES) & (spread_row // 2 == spread_lane % 8))

    shape = (16, HALF)
    col = iota(shape, 1)
    even_col = col % 2 == 0
    is_real = iota(shape, 0) % 2 == 0

    def times_unit(values):
        return jnp.where(is_real, -pltpu.roll(values, 15, 0), pltpu.roll(values, 1, 0))

    def neighbours(slot, values):
        wave, last = waves[slot]
        flow = jnp.where(even_col, values[:16], values[16:])
        flow = jnp.where(wave + col <= last, flow, 0.0)
        before = jnp.where(col == 0, 0.0, pltpu.roll(flow, 1, 1))
        after = jnp.where(col == HALF - 1, 0.0, pltpu.roll(flow, HALF - 1, 1))
        return before, flow, after

    waves = []
    for slot in range(4):
        hits = ((owner_ref[...] == me) & (rank == float(slot))).astype(F32)
        used = jnp.sum(hits)
        wave = jnp.where(used > 0, jnp.sum(hits * window), float(HALF)).astype(I32)
        waves.append((wave, jnp.where(used > 0, 2 * HALF - 1, -1)))
        degree_row = wave + iota((8, HALF), 1)
        degree = degree_row.astype(F32)
        next_row = degree_row + 1
        squared = wave * wave
        eps_here = jnp.sqrt((degree_row * degree_row - squared).astype(F32) / (4.0 * degree * degree - 1.0))
        eps_next = jnp.sqrt(
            (next_row * next_row - squared).astype(F32) / (4.0 * (degree + 1.0) * (degree + 1.0) - 1.0)
        )
        factor = lax.rsqrt(degree * (degree + 1.0))
        terms[slot, 0] = (degree + 1.0) * eps_here * factor
        terms[slot, 1] = degree * eps_next * factor
        terms[slot, 2] = wave.astype(F32) * factor
    summed[...] = jnp.zeros_like(summed)

    arrive(0)
    turned = turn(0)
    for slot in range(4):
        table_ready(slot)
        before, flow, after = neighbours(slot, project(turned, slot))
        partial[slot, 0] = terms[slot, 0, :1] * before - terms[slot, 1, :1] * after
        partial[slot, 1] = terms[slot, 2, :1] * times_unit(flow)

    own_levels = pl.ds(core * 8, 8)

    def hand_over(slot):
        return pltpu.make_async_remote_copy(
            src_ref=coeffs_out.at[slot], dst_ref=coeffs.at[slot, :, own_levels],
            send_sem=coeffs_send.at[slot], recv_sem=coeffs_recv.at[slot],
            device_id=(me, other), device_id_type=MESH,
        )

    arrive(1)
    turned = turn(1)
    for slot in range(4):
        wave, last = waves[slot]
        live = wave + col <= last
        before, flow, after = neighbours(slot, project(turned, slot))
        vorticity = partial[slot, 0] + terms[slot, 2, :1] * times_unit(flow)
        divergence = partial[slot, 1] - terms[slot, 0, :1] * before + terms[slot, 1, :1] * after
        vorticity = jnp.where(live, vorticity, 0.0)
        divergence = jnp.where(live, divergence, 0.0)
        for q, values in enumerate((vorticity, divergence)):
            lower, upper = values[:, :COLS], values[:, COLS:]
            coeffs[slot, q, own_levels] = jnp.where(core == 0, lower, upper).reshape(8, 2, COLS)
            coeffs_out[slot, q] = jnp.where(core == 0, upper, lower).reshape(8, 2, COLS)
        hand_over(slot).start()
        vorticity = vorticity * vorticity
        divergence = divergence * divergence
        energy = jnp.where(
            is_real,
            vorticity + pltpu.roll(vorticity, 15, 0),
            divergence + pltpu.roll(divergence, 1, 0),
        )
        summed[...] += pltpu.roll(energy, wave - HALF, 1)

    upright = jnp.transpose(summed[...], (1, 0)).astype(BF16)
    placed = jnp.dot(upright, spread, preferred_element_type=F32).astype(BF16) * fold_mask[...]
    messages = jnp.dot(fold_rows[...], placed, preferred_element_type=F32)
    for half in range(2):
        fold_out[:, half, :] = messages[:, LANES * half : LANES * half + LANES]
    fold_in[me] = fold_out[me]

    def send_fold(target, index):
        pltpu.make_async_remote_copy(
            src_ref=fold_out.at[target], dst_ref=fold_in.at[me],
            send_sem=fold_sems.at[0], recv_sem=fold_sems.at[1],
            device_id=(target, core), device_id_type=MESH,
        ).start()

    everyone(send_fold)
    arrived = fold_in.at[pl.ds(0, 127)]
    pltpu.make_async_copy(arrived, arrived, fold_sems.at[1]).wait()
    lines = fold_in.reshape(2 * LANES, LANES)
    folded = lines[0:8, :]
    for index in range(1, 32):
        folded = folded + lines[8 * index : 8 * index + 8, :]
    final[core] = folded[0:2] + folded[2:4] + folded[4:6] + folded[6:8]
    swap = pltpu.make_async_remote_copy(
        src_ref=final.at[core], dst_ref=final.at[core],
        send_sem=final_sems.at[0], recv_sem=final_sems.at[1],
        device_id=(me, other), device_id_type=MESH,
    )
    swap.start()
    for f in range(2):
        sent = outgoing.at[f, pl.ds(0, 127)]
        pltpu.make_async_copy(sent, sent, out_sems.at[f]).wait()
    for slot in range(4):
        table_share(slot).wait_send()
        hand_over(slot).wait_send()
        half = coeffs.at[slot, :, pl.ds(other * 8, 8)]
        pltpu.make_async_copy(half, half, coeffs_recv.at[slot]).wait()
    sent = fold_out.at[pl.ds(0, 127)]
    pltpu.make_async_copy(sent, sent, fold_sems.at[0]).wait()
    swap.wait()
    halves = []
    for half in range(2):
        values = final[half] * (1.0 / ENTRIES)
        halves.append(jnp.where(core == 1, pltpu.roll(values, 64, 1), values))
    for index in range(5):
        spectra_ref[index] = stack([values[:, 8 * index : 8 * index + 8] for values in halves], 1)


def tiles(wind):
    split = wind.transpose(0, 2, 1, 3).reshape(8, ROWS, 2, COARSE, LANES)
    return split.transpose(0, 1, 3, 2, 4).reshape(80, COARSE, 2, LANES)


def local(wind_u, wind_v, window_m, owner, legendre):
    vmem = pl.BlockSpec(memory_space=pltpu.VMEM)
    hbm = pl.BlockSpec(memory_space=pl.ANY)
    dma = pltpu.SemaphoreType.DMA
    coeffs, spectra = pl.pallas_call(
        kernel,
        out_shape=(pltpu.VMEM((4, 2, 16, 2, COLS), F32), pltpu.VMEM((5, 2, 16), F32)),
        in_specs=[hbm, hbm, vmem, vmem, hbm],
        out_specs=(vmem, vmem),
        scratch_shapes=[
            pltpu.VMEM((2, COARSE, 80, 2, LANES), BF16),
            pltpu.VMEM((COARSE, ENTRIES), F32),
            pltpu.VMEM((COARSE, ENTRIES), F32),
            pltpu.VMEM((LANES, ENTRIES), F32),
            pltpu.VMEM((LANES, ENTRIES), F32),
            pltpu.VMEM((2 * NLON, 2 * ENTRIES), BF16),
            pltpu.VMEM((160, 2 * ENTRIES), F32),
            pltpu.VMEM((4, 192, LANES), F32),
            pltpu.VMEM((2, 128, 5, 2, LANES), BF16),
            pltpu.VMEM((2, 8, 16, 5, 2, LANES), BF16),
            pltpu.VMEM((4, HALF, HALF), BF16),
            pltpu.VMEM((4, 3, 8, HALF), F32),
            pltpu.VMEM((4, 2, 16, HALF), F32),
            pltpu.VMEM((16, HALF), F32),
            pltpu.VMEM((4, 2, 8, 2, COLS), F32),
            pltpu.VMEM((HALF, 2 * LANES), BF16),
            pltpu.VMEM((LANES, HALF), BF16),
            pltpu.VMEM((LANES, 2, LANES), F32),
            pltpu.VMEM((LANES, 2, LANES), F32),
            pltpu.VMEM((2, 2, LANES), F32),
            dma((2, STEPS)), dma((4,)), dma((4,)), dma((4,)), pltpu.SemaphoreType.REGULAR,
            dma((2,)), dma((2, 16)), dma((4,)), dma((4,)), dma((2,)), dma((2,)),
        ],
        compiler_params=pltpu.CompilerParams(
            collective_id=0, has_side_effects=True, vmem_limit_bytes=VMEM_BYTES
        ),
    )(tiles(wind_u), tiles(wind_v), window_m[None, :], owner[None, :], legendre)
    return (coeffs, spectra.transpose(1, 2, 0))


def solution(mesh):
    placed = (
        P("deg", None, "wave", None),
        P("deg", None, "wave", None),
        P(),
        P(),
        P("wave", None, "deg"),
    )
    return jax.shard_map(
        local,
        mesh=mesh,
        in_specs=placed,
        out_specs=(P("wave", None, None, None, "deg"), P(None, None, ("wave", "deg"))),
        check_vma=False,
    )
```

```python
import math

import jax
import jax.numpy as jnp
from jax import lax
from jax.experimental import pallas as pl
from jax.experimental.pallas import tpu as pltpu
from jax.sharding import PartitionSpec as P

MESH = pl.DeviceIdType.MESH
BF16 = jnp.bfloat16
F32 = jnp.float32
I32 = jnp.int32
VMEM_BYTES = 56 * 1024 * 1024

NLON = 5120
LANES = 128
COARSE = NLON // LANES
ENTRIES = 256
ROWS = 10
HALF = 1280
COLS = 640
CHUNK = 20
STEPS = COARSE // CHUNK

NT = (((1,), (1,)), ((), ()))
FAR_PLANES = (4, 3, 5, 2, 6, 1, 7, 0)
FAR_LINES = (2, 1, 3, 0)


def iota(shape, axis):
    return lax.broadcasted_iota(I32, shape, axis)


def one_hot(hits):
    return hits.astype(F32).astype(BF16)


def row_order():
    wanted = iota((320, 320), 0)
    source = wanted % 2 * 160 + wanted // 16 % 2 * 80 + wanted // 2 % 8 * 10 + wanted // 32
    return one_hot(source == iota((320, 320), 1))


def group_order():
    source = iota((160, 160), 1)
    return one_hot(source % 16 * ROWS + source // 16 == iota((160, 160), 0))


def unit_waves(count, window, period):
    phase = iota((count, ENTRIES), 0).astype(F32) * window
    phase = phase - period * jnp.round(phase * (1.0 / period))
    angle = phase * (2.0 * math.pi / period)
    return jnp.cos(angle), jnp.sin(angle)


def stack(pieces, axis):
    return jnp.concatenate(pieces, axis=axis)


def kernel(
    wind_u, wind_v, window_ref, owner_ref, table_hbm, coeffs, spectra_ref,
    winds, coarse_cos, coarse_sin, fine_cos, fine_sin, waves_table, total, split,
    outgoing, data, table, terms, partial, summed, coeffs_out,
    fold_mask, fold_rows, fold_out, fold_in, final,
    wind_sems, table_sems, share_send, share_recv, meet,
    out_sems, in_sems, coeffs_send, coeffs_recv, fold_sems, final_sems,
):
    me = lax.axis_index("wave")
    core = lax.axis_index("deg")
    other = 1 - core
    plane = me // 16
    inside = me % 16
    row = inside // 4
    column = inside % 4

    planes = [(plane + away) % 8 * 16 for away in FAR_PLANES]

    def group_base(index):
        turn_x = index // 4
        turn_y = index % 4
        away_x = 2 + (turn_x + 1) // 2 * (1 - 2 * (turn_x % 2))
        away_y = 2 + (turn_y + 1) // 2 * (1 - 2 * (turn_y % 2))
        return (row + away_x) % 4 * 4 + (column + away_y) % 4

    def everyone(action):
        def group(index, carry):
            base = group_base(index)
            for start in planes:
                action(start + base, index)
            return carry

        lax.fori_loop(0, 15, group, 0)
        for start in planes[:7]:
            action(start + inside, 15)

    def wind_copy(f, tile):
        ref = (wind_u, wind_v)[f]
        return pltpu.make_async_copy(ref.at[:, tile], winds.at[f, tile], wind_sems.at[f, tile // CHUNK])

    for tile in range(COARSE):
        wind_copy(0, tile).start()
    def greet_plane(sem):
        def greet(step, carry):
            there = plane * 16 + (inside + step) % 16
            pl.semaphore_signal(sem, inc=1, device_id=(there, core), device_id_type=MESH)
            return carry

        lax.fori_loop(1, 16, greet, 0)

    def greet_line(step, carry):
        there = (plane + step) % 8 * 16 + inside
        pl.semaphore_signal(barrier, inc=1, device_id=(there, core), device_id_type=MESH)
        return carry

    barrier = pltpu.get_barrier_semaphore()
    pl.semaphore_signal(barrier, inc=1, device_id=(me, other), device_id_type=MESH)
    lax.fori_loop(1, 8, greet_line, 0)
    greet_plane(barrier)

    own_half = pl.ds(pl.multiple_of(core * COLS, LANES), COLS)

    def table_copy(slot):
        return pltpu.make_async_copy(table_hbm.at[slot], table.at[slot, :, own_half], table_sems.at[slot])

    def table_share(slot):
        return pltpu.make_async_remote_copy(
            src_ref=table_hbm.at[slot], dst_ref=table.at[slot, :, own_half],
            send_sem=share_send.at[slot], recv_sem=share_recv.at[slot],
            device_id=(me, other), device_id_type=MESH,
        )

    def table_ready(slot):
        table_copy(slot).wait()
        half = table.at[slot, :, pl.ds(pl.multiple_of(other * COLS, LANES), COLS)]
        pltpu.make_async_copy(half, half, share_recv.at[slot]).wait()

    window = window_ref[...].astype(F32)
    cos_part, sin_part = unit_waves(COARSE, window, float(COARSE))
    coarse_cos[...] = cos_part
    coarse_sin[...] = sin_part
    cos_part, sin_part = unit_waves(LANES, window, float(NLON))
    fine_cos[...] = cos_part * (1.0 / NLON)
    fine_sin[...] = sin_part * (1.0 / NLON)

    def wind_chunk(f, chunk):
        part = winds.at[f, pl.ds(chunk * CHUNK, CHUNK)]
        pltpu.make_async_copy(part, part, wind_sems.at[f, chunk]).wait()
        return stack(
            [winds.at[f, chunk * CHUNK + inner].reshape(160, LANES)[...] for inner in range(CHUNK)], 1
        )

    def prepare(step, carry):
        cos_b = fine_cos[...]
        sin_b = fine_sin[...]
        for inner in range(5):
            tile = step * 5 + inner
            wind_copy(1, tile).start()
            cos_a = coarse_cos[pl.ds(tile, 1), :]
            sin_a = coarse_sin[pl.ds(tile, 1), :]
            values = stack([cos_a * cos_b - sin_a * sin_b, -(sin_a * cos_b + cos_a * sin_b)], 1)
            high = values.astype(BF16)
            first = (tile // CHUNK * CHUNK + tile) * LANES
            waves_table[pl.ds(pl.multiple_of(first, LANES), LANES), :] = high
            second = first + CHUNK * LANES
            low = (values - high.astype(F32)).astype(BF16)
            waves_table[pl.ds(pl.multiple_of(second, LANES), LANES), :] = low
        return carry

    def transform(f):
        def step(chunk):
            part = wind_chunk(f, chunk)
            depth = 2 * CHUNK * LANES
            product = jnp.dot(
                stack([part, part], 1),
                waves_table[depth * chunk : depth * chunk + depth, :],
                preferred_element_type=F32,
            )
            if chunk == 0:
                total[...] = product
            else:
                total[...] += product

        for chunk in range(STEPS):
            step(chunk)

    def publish(f):
        for tile in range(4):
            split[tile, :160] = total[:, LANES * tile : LANES * tile + LANES]
        north = stack([split[tile, pl.ds(0, 80, stride=2), :] for tile in range(4)], 1)
        south = stack([split[tile, pl.ds(1, 80, stride=2), :] for tile in range(4)], 1)
        even = (north + south).astype(BF16)
        odd = (north - south).astype(BF16)
        paired = stack([even[:, :ENTRIES], odd[:, :ENTRIES], even[:, ENTRIES:], odd[:, ENTRIES:]], 0)
        ordered = jnp.dot(row_order(), paired, preferred_element_type=F32).astype(BF16)
        blocks = stack(
            [
                ordered[32 * line : 32 * line + 32] * rank_masks[slot]
                for line in range(ROWS)
                for slot in range(4)
            ],
            0,
        )
        placed = lax.dot_general(placing, blocks, NT, preferred_element_type=F32).astype(BF16)
        stacked = stack(
            [
                stack(
                    [placed[16 * g : 16 * g + 16, LANES * line : LANES * line + LANES] for g in range(8)], 1
                )
                for line in range(ROWS)
            ],
            0,
        )
        result = jnp.dot(group_order(), stacked, preferred_element_type=F32).astype(BF16)
        flat = outgoing.at[f].reshape(HALF, LANES)
        for g in range(8):
            flat[160 * g : 160 * g + 160, :] = result[:, LANES * g : LANES * g + LANES]

    def own_copy(f):
        return pltpu.make_async_copy(
            outgoing.at[f, me], data.at[f, plane, inside], in_sems.at[f, 15]
        )

    def send_all(f):
        own_copy(f).start()

        def send(target, index):
            pltpu.make_async_remote_copy(
                src_ref=outgoing.at[f, target], dst_ref=data.at[f, plane, inside],
                send_sem=out_sems.at[f], recv_sem=in_sems.at[f, index],
                device_id=(target, core), device_id_type=MESH,
            ).start()

        everyone(send)

    def arrive(f):
        for step in range(16):
            source = (row + 4 - FAR_LINES[step // 4]) % 4 * 4 + (column + 4 - FAR_LINES[step % 4]) % 4
            part = data.at[f, :, source]
            pltpu.make_async_copy(part, part, in_sems.at[f, step]).wait()

    unit = one_hot(iota((LANES, LANES), 0) == iota((LANES, LANES), 1))

    def turn(f):
        return lax.dot_general(
            unit, data.at[f].reshape(HALF, LANES)[...], NT, preferred_element_type=F32
        ).astype(BF16)

    def project(turned, slot):
        return jnp.dot(turned[32 * slot : 32 * slot + 32], table[slot], preferred_element_type=F32)

    lax.fori_loop(0, 4, prepare, 0)
    pl.semaphore_wait(barrier, 23)
    greet_plane(meet)
    lax.fori_loop(4, 8, prepare, 0)
    owner = owner_ref[...].astype(F32)
    owner_rows = jnp.broadcast_to(owner, (ENTRIES, ENTRIES))
    same = (jnp.transpose(owner_rows, (1, 0)) == owner_rows) & (
        iota((ENTRIES, ENTRIES), 0) < iota((ENTRIES, ENTRIES), 1)
    )
    rank = jnp.sum(same.astype(F32), axis=0, keepdims=True)
    placing = one_hot(owner_ref[...] == iota((128, ENTRIES), 0))
    rank_masks = [one_hot(rank == float(slot)) for slot in range(4)]

    transform(0)
    publish(0)
    pl.semaphore_wait(meet, 15)
    send_all(0)
    for slot in range(4):
        table_copy(slot).start()

    transform(1)
    publish(1)
    send_all(1)
    for slot in range(4):
        table_share(slot).start()

    fold_lane = iota((HALF, 2 * LANES), 1)
    fold_turn = fold_lane % 64 // 8
    fold_mask[...] = one_hot(
        (iota((HALF, 2 * LANES), 0) % 10 == fold_lane % LANES // 64 * 5 + fold_turn) & (fold_turn < 5)
    )
    fold_rows[...] = one_hot(iota((LANES, HALF), 1) // 10 == iota((LANES, HALF), 0))
    pair_row = iota((2 * LANES, 2 * LANES), 0)
    interleave = one_hot(pair_row % 2 * LANES + pair_row // 2 == iota((2 * LANES, 2 * LANES), 1))
    spread_row = iota((16, 2 * LANES), 0)
    spread_lane = iota((16, 2 * LANES), 1)
    spread = one_hot((spread_row % 2 == spread_lane // LANES) & (spread_row // 2 == spread_lane % 8))

    shape = (16, HALF)
    col = iota(shape, 1)
    even_col = col % 2 == 0
    is_real = iota(shape, 0) % 2 == 0

    def times_unit(values):
        return jnp.where(is_real, -pltpu.roll(values, 15, 0), pltpu.roll(values, 1, 0))

    def neighbours(slot, values):
        wave, last = waves[slot]
        flow = jnp.where(even_col, values[:16], values[16:])
        flow = jnp.where(wave + col <= last, flow, 0.0)
        before = jnp.where(col == 0, 0.0, pltpu.roll(flow, 1, 1))
        after = jnp.where(col == HALF - 1, 0.0, pltpu.roll(flow, HALF - 1, 1))
        return before, flow, after

    waves = []
    for slot in range(4):
        hits = ((owner_ref[...] == me) & (rank == float(slot))).astype(F32)
        used = jnp.sum(hits)
        wave = jnp.where(used > 0, jnp.sum(hits * window), float(HALF)).astype(I32)
        waves.append((wave, jnp.where(used > 0, 2 * HALF - 1, -1)))
        degree_row = wave + iota((8, HALF), 1)
        degree = degree_row.astype(F32)
        next_row = degree_row + 1
        squared = wave * wave
        eps_here = jnp.sqrt((degree_row * degree_row - squared).astype(F32) / (4.0 * degree * degree - 1.0))
        eps_next = jnp.sqrt(
            (next_row * next_row - squared).astype(F32) / (4.0 * (degree + 1.0) * (degree + 1.0) - 1.0)
        )
        factor = lax.rsqrt(degree * (degree + 1.0))
        terms[slot, 0] = (degree + 1.0) * eps_here * factor
        terms[slot, 1] = degree * eps_next * factor
        terms[slot, 2] = wave.astype(F32) * factor
    summed[...] = jnp.zeros_like(summed)

    arrive(0)
    turned = turn(0)
    for slot in range(4):
        table_ready(slot)
        before, flow, after = neighbours(slot, project(turned, slot))
        partial[slot, 0] = terms[slot, 0, :1] * before - terms[slot, 1, :1] * after
        partial[slot, 1] = terms[slot, 2, :1] * times_unit(flow)

    own_levels = pl.ds(core * 8, 8)

    def hand_over(slot):
        return pltpu.make_async_remote_copy(
            src_ref=coeffs_out.at[slot], dst_ref=coeffs.at[slot, :, own_levels],
            send_sem=coeffs_send.at[slot], recv_sem=coeffs_recv.at[slot],
            device_id=(me, other), device_id_type=MESH,
        )

    arrive(1)
    turned = turn(1)
    for slot in range(4):
        wave, last = waves[slot]
        live = wave + col <= last
        before, flow, after = neighbours(slot, project(turned, slot))
        vorticity = partial[slot, 0] + terms[slot, 2, :1] * times_unit(flow)
        divergence = partial[slot, 1] - terms[slot, 0, :1] * before + terms[slot, 1, :1] * after
        vorticity = jnp.where(live, vorticity, 0.0)
        divergence = jnp.where(live, divergence, 0.0)
        for q, values in enumerate((vorticity, divergence)):
            lower, upper = values[:, :COLS], values[:, COLS:]
            coeffs[slot, q, own_levels] = jnp.where(core == 0, lower, upper).reshape(8, 2, COLS)
            coeffs_out[slot, q] = jnp.where(core == 0, upper, lower).reshape(8, 2, COLS)
        hand_over(slot).start()
        vorticity = vorticity * vorticity
        divergence = divergence * divergence
        energy = jnp.where(
            is_real,
            vorticity + pltpu.roll(vorticity, 15, 0),
            divergence + pltpu.roll(divergence, 1, 0),
        )
        summed[...] += pltpu.roll(energy, wave - HALF, 1)

    upright = jnp.transpose(summed[...], (1, 0)).astype(BF16)
    placed = jnp.dot(upright, spread, preferred_element_type=F32).astype(BF16) * fold_mask[...]
    messages = jnp.dot(fold_rows[...], placed, preferred_element_type=F32)
    messages = messages.astype(BF16)
    messages = stack([messages[:, :LANES], messages[:, LANES:]], 0)
    fold_out.reshape(2 * LANES, LANES)[...] = jnp.dot(
        interleave, messages, preferred_element_type=F32
    ).astype(BF16)
    fold_in[me] = fold_out[me]

    def send_fold(target, index):
        pltpu.make_async_remote_copy(
            src_ref=fold_out.at[target], dst_ref=fold_in.at[me],
            send_sem=fold_sems.at[0], recv_sem=fold_sems.at[1],
            device_id=(target, core), device_id_type=MESH,
        ).start()

    everyone(send_fold)
    arrived = fold_in.at[pl.ds(0, 127)]
    pltpu.make_async_copy(arrived, arrived, fold_sems.at[1]).wait()
    lines = fold_in.reshape(2 * LANES, LANES)[...].astype(F32)
    folded = lines[0:8]
    for index in range(1, 32):
        folded = folded + lines[8 * index : 8 * index + 8]
    final[core] = folded[0:2] + folded[2:4] + folded[4:6] + folded[6:8]
    swap = pltpu.make_async_remote_copy(
        src_ref=final.at[core], dst_ref=final.at[core],
        send_sem=final_sems.at[0], recv_sem=final_sems.at[1],
        device_id=(me, other), device_id_type=MESH,
    )
    swap.start()
    for f in range(2):
        sent = outgoing.at[f, pl.ds(0, 127)]
        pltpu.make_async_copy(sent, sent, out_sems.at[f]).wait()
    for slot in range(4):
        table_share(slot).wait_send()
        hand_over(slot).wait_send()
        half = coeffs.at[slot, :, pl.ds(other * 8, 8)]
        pltpu.make_async_copy(half, half, coeffs_recv.at[slot]).wait()
    sent = fold_out.at[pl.ds(0, 127)]
    pltpu.make_async_copy(sent, sent, fold_sems.at[0]).wait()
    swap.wait()
    halves = []
    for half in range(2):
        values = final[half] * (1.0 / ENTRIES)
        halves.append(jnp.where(core == 1, pltpu.roll(values, 64, 1), values))
    for index in range(5):
        spectra_ref[index] = stack([values[:, 8 * index : 8 * index + 8] for values in halves], 1)


def tiles(wind):
    split = wind.transpose(0, 2, 1, 3).reshape(8, ROWS, 2, COARSE, LANES)
    return split.transpose(0, 1, 3, 2, 4).reshape(80, COARSE, 2, LANES)


def local(wind_u, wind_v, window_m, owner, legendre):
    vmem = pl.BlockSpec(memory_space=pltpu.VMEM)
    hbm = pl.BlockSpec(memory_space=pl.ANY)
    dma = pltpu.SemaphoreType.DMA
    coeffs, spectra = pl.pallas_call(
        kernel,
        out_shape=(pltpu.VMEM((4, 2, 16, 2, COLS), F32), pltpu.VMEM((5, 2, 16), F32)),
        in_specs=[hbm, hbm, vmem, vmem, hbm],
        out_specs=(vmem, vmem),
        scratch_shapes=[
            pltpu.VMEM((2, COARSE, 80, 2, LANES), BF16),
            pltpu.VMEM((COARSE, ENTRIES), F32),
            pltpu.VMEM((COARSE, ENTRIES), F32),
            pltpu.VMEM((LANES, ENTRIES), F32),
            pltpu.VMEM((LANES, ENTRIES), F32),
            pltpu.VMEM((2 * NLON, 2 * ENTRIES), BF16),
            pltpu.VMEM((160, 2 * ENTRIES), F32),
            pltpu.VMEM((4, 192, LANES), F32),
            pltpu.VMEM((2, 128, 5, 2, LANES), BF16),
            pltpu.VMEM((2, 8, 16, 5, 2, LANES), BF16),
            pltpu.VMEM((4, HALF, HALF), BF16),
            pltpu.VMEM((4, 3, 8, HALF), F32),
            pltpu.VMEM((4, 2, 16, HALF), F32),
            pltpu.VMEM((16, HALF), F32),
            pltpu.VMEM((4, 2, 8, 2, COLS), F32),
            pltpu.VMEM((HALF, 2 * LANES), BF16),
            pltpu.VMEM((LANES, HALF), BF16),
            pltpu.VMEM((LANES, 2, LANES), BF16),
            pltpu.VMEM((LANES, 2, LANES), BF16),
            pltpu.VMEM((2, 2, LANES), F32),
            dma((2, STEPS)), dma((4,)), dma((4,)), dma((4,)), pltpu.SemaphoreType.REGULAR,
            dma((2,)), dma((2, 16)), dma((4,)), dma((4,)), dma((2,)), dma((2,)),
        ],
        compiler_params=pltpu.CompilerParams(
            collective_id=0, has_side_effects=True, vmem_limit_bytes=VMEM_BYTES
        ),
    )(tiles(wind_u), tiles(wind_v), window_m[None, :], owner[None, :], legendre)
    return (coeffs, spectra.transpose(1, 2, 0))


def solution(mesh):
    placed = (
        P("deg", None, "wave", None),
        P("deg", None, "wave", None),
        P(),
        P(),
        P("wave", None, "deg"),
    )
    return jax.shard_map(
        local,
        mesh=mesh,
        in_specs=placed,
        out_specs=(P("wave", None, None, None, "deg"), P(None, None, ("wave", "deg"))),
        check_vma=False,
    )
```

```python
import math

import jax
import jax.numpy as jnp
from jax import lax
from jax.experimental import pallas as pl
from jax.experimental.pallas import tpu as pltpu
from jax.sharding import PartitionSpec as P

MESH = pl.DeviceIdType.MESH
BF16 = jnp.bfloat16
F32 = jnp.float32
I32 = jnp.int32
VMEM_BYTES = 56 * 1024 * 1024

NLON = 5120
LANES = 128
COARSE = NLON // LANES
ENTRIES = 256
ROWS = 10
HALF = 1280
COLS = 640
CHUNK = 20
STEPS = COARSE // CHUNK

NT = (((1,), (1,)), ((), ()))
BATCHES = ((0, 0, 4), (0, 4, 6), (1, 0, 10))
FAR_PLANES = (4, 3, 5, 2, 6, 1, 7, 0)
FAR_LINES = (2, 1, 3, 0)


def iota(shape, axis):
    return lax.broadcasted_iota(I32, shape, axis)


def one_hot(hits):
    return hits.astype(F32).astype(BF16)


def row_order(rows):
    wanted = iota((32 * rows, 32 * rows), 0)
    source = (
        wanted % 2 * (16 * rows) + wanted // 16 % 2 * (8 * rows) + wanted // 2 % 8 * rows + wanted // 32
    )
    return one_hot(source == iota((32 * rows, 32 * rows), 1))


def group_order(rows):
    source = iota((16 * rows, 16 * rows), 1)
    return one_hot(source % 16 * rows + source // 16 == iota((16 * rows, 16 * rows), 0))


def unit_waves(count, window, period):
    phase = iota((count, ENTRIES), 0).astype(F32) * window
    phase = phase - period * jnp.round(phase * (1.0 / period))
    angle = phase * (2.0 * math.pi / period)
    return jnp.cos(angle), jnp.sin(angle)


def stack(pieces, axis):
    return jnp.concatenate(pieces, axis=axis)


def kernel(
    wind_u, wind_v, window_ref, owner_ref, table_hbm, coeffs, spectra_ref,
    winds_a, winds_b, winds_c, coarse_cos, coarse_sin, fine_cos, fine_sin, waves_table, total, split,
    outgoing_a, outgoing_b, outgoing_c, data, table, terms, partial, summed, coeffs_out,
    fold_mask, fold_rows, fold_out, fold_in, final,
    wind_sems, table_sems, share_send, share_recv, meet,
    out_sems, in_sems, coeffs_send, coeffs_recv, fold_sems, final_sems,
):
    winds = (winds_a, winds_b, winds_c)
    outgoing = (outgoing_a, outgoing_b, outgoing_c)
    me = lax.axis_index("wave")
    core = lax.axis_index("deg")
    other = 1 - core
    plane = me // 16
    inside = me % 16
    row = inside // 4
    column = inside % 4

    planes = [(plane + away) % 8 * 16 for away in FAR_PLANES]

    def group_base(index):
        turn_x = index // 4
        turn_y = index % 4
        away_x = 2 + (turn_x + 1) // 2 * (1 - 2 * (turn_x % 2))
        away_y = 2 + (turn_y + 1) // 2 * (1 - 2 * (turn_y % 2))
        return (row + away_x) % 4 * 4 + (column + away_y) % 4

    def everyone(action):
        def group(index, carry):
            base = group_base(index)
            for start in planes:
                action(start + base, index)
            return carry

        lax.fori_loop(0, 15, group, 0)
        for start in planes[:7]:
            action(start + inside, 15)

    def wind_copy(batch, tile):
        f, first, rows = BATCHES[batch]
        ref = (wind_u, wind_v)[f]
        return pltpu.make_async_copy(
            ref.at[:, pl.ds(first, rows), tile], winds[batch].at[tile], wind_sems.at[batch, tile // CHUNK]
        )

    for tile in range(COARSE):
        wind_copy(0, tile).start()
    def greet_plane(sem):
        def greet(step, carry):
            there = plane * 16 + (inside + step) % 16
            pl.semaphore_signal(sem, inc=1, device_id=(there, core), device_id_type=MESH)
            return carry

        lax.fori_loop(1, 16, greet, 0)

    def greet_line(step, carry):
        there = (plane + step) % 8 * 16 + inside
        pl.semaphore_signal(barrier, inc=1, device_id=(there, core), device_id_type=MESH)
        return carry

    barrier = pltpu.get_barrier_semaphore()
    pl.semaphore_signal(barrier, inc=1, device_id=(me, other), device_id_type=MESH)
    lax.fori_loop(1, 8, greet_line, 0)
    greet_plane(barrier)

    own_half = pl.ds(pl.multiple_of(core * COLS, LANES), COLS)

    def table_copy(slot):
        return pltpu.make_async_copy(table_hbm.at[slot], table.at[slot, :, own_half], table_sems.at[slot])

    def table_share(slot):
        return pltpu.make_async_remote_copy(
            src_ref=table_hbm.at[slot], dst_ref=table.at[slot, :, own_half],
            send_sem=share_send.at[slot], recv_sem=share_recv.at[slot],
            device_id=(me, other), device_id_type=MESH,
        )

    def table_ready(slot):
        table_copy(slot).wait()
        half = table.at[slot, :, pl.ds(pl.multiple_of(other * COLS, LANES), COLS)]
        pltpu.make_async_copy(half, half, share_recv.at[slot]).wait()

    window = window_ref[...].astype(F32)
    owner = owner_ref[...].astype(F32)
    owner_rows = jnp.broadcast_to(owner, (ENTRIES, ENTRIES))
    same = (jnp.transpose(owner_rows, (1, 0)) == owner_rows) & (
        iota((ENTRIES, ENTRIES), 0) < iota((ENTRIES, ENTRIES), 1)
    )
    rank = jnp.sum(same.astype(F32), axis=0, keepdims=True)
    placing = one_hot(owner_ref[...] == iota((128, ENTRIES), 0))
    rank_masks = [one_hot(rank == float(slot)) for slot in range(4)]

    cos_part, sin_part = unit_waves(COARSE, window, float(COARSE))
    coarse_cos[...] = cos_part
    coarse_sin[...] = sin_part
    cos_part, sin_part = unit_waves(LANES, window, float(NLON))
    fine_cos[...] = cos_part * (1.0 / NLON)
    fine_sin[...] = sin_part * (1.0 / NLON)

    def wind_chunk(batch, chunk):
        lines = 16 * BATCHES[batch][2]
        part = winds[batch].at[pl.ds(chunk * CHUNK, CHUNK)]
        pltpu.make_async_copy(part, part, wind_sems.at[batch, chunk]).wait()
        return stack(
            [winds[batch].at[chunk * CHUNK + inner].reshape(lines, LANES)[...] for inner in range(CHUNK)], 1
        )

    def prepare(step, carry):
        cos_b = fine_cos[...]
        sin_b = fine_sin[...]
        for inner in range(5):
            tile = step * 5 + inner
            wind_copy(1, tile).start()
            wind_copy(2, tile).start()
            cos_a = coarse_cos[pl.ds(tile, 1), :]
            sin_a = coarse_sin[pl.ds(tile, 1), :]
            values = stack([cos_a * cos_b - sin_a * sin_b, -(sin_a * cos_b + cos_a * sin_b)], 1)
            high = values.astype(BF16)
            first = (tile // CHUNK * CHUNK + tile) * LANES
            waves_table[pl.ds(pl.multiple_of(first, LANES), LANES), :] = high
            second = first + CHUNK * LANES
            low = (values - high.astype(F32)).astype(BF16)
            waves_table[pl.ds(pl.multiple_of(second, LANES), LANES), :] = low
        return carry

    def transform(batch):
        here_rows = slice(0, 16 * BATCHES[batch][2])

        def step(chunk, carry):
            part = wind_chunk(batch, chunk)
            depth = 2 * CHUNK * LANES
            here = pl.ds(pl.multiple_of(chunk * depth, depth), depth)
            total[here_rows, :] += jnp.dot(
                stack([part, part], 1), waves_table[here, :], preferred_element_type=F32
            )
            return carry

        total[here_rows, :] = jnp.zeros((16 * BATCHES[batch][2], 2 * ENTRIES), F32)
        lax.fori_loop(0, STEPS, step, 0)

    def publish(batch):
        rows = BATCHES[batch][2]
        lines = 16 * rows
        for tile in range(4):
            split[tile, :lines] = total[:lines, LANES * tile : LANES * tile + LANES]
        north = stack([split[tile, pl.ds(0, 8 * rows, stride=2), :] for tile in range(4)], 1)
        south = stack([split[tile, pl.ds(1, 8 * rows, stride=2), :] for tile in range(4)], 1)
        even = (north + south).astype(BF16)
        odd = (north - south).astype(BF16)
        paired = stack([even[:, :ENTRIES], odd[:, :ENTRIES], even[:, ENTRIES:], odd[:, ENTRIES:]], 0)
        ordered = jnp.dot(row_order(rows), paired, preferred_element_type=F32).astype(BF16)
        blocks = stack(
            [
                ordered[32 * line : 32 * line + 32] * rank_masks[slot]
                for line in range(rows)
                for slot in range(4)
            ],
            0,
        )
        placed = lax.dot_general(placing, blocks, NT, preferred_element_type=F32).astype(BF16)
        stacked = stack(
            [
                stack(
                    [placed[16 * g : 16 * g + 16, LANES * line : LANES * line + LANES] for g in range(8)], 1
                )
                for line in range(rows)
            ],
            0,
        )
        result = jnp.dot(group_order(rows), stacked, preferred_element_type=F32).astype(BF16)
        flat = outgoing[batch].reshape(LANES * rows, LANES)
        for g in range(8):
            flat[lines * g : lines * g + lines, :] = result[:, LANES * g : LANES * g + LANES]

    def send_all(batch):
        f, first, rows = BATCHES[batch]
        place = data.at[f, plane, inside, pl.ds(first // 2, rows // 2)]
        pltpu.make_async_copy(outgoing[batch].at[me], place, in_sems.at[batch, 15]).start()

        def send(target, index):
            pltpu.make_async_remote_copy(
                src_ref=outgoing[batch].at[target], dst_ref=place,
                send_sem=out_sems.at[batch], recv_sem=in_sems.at[batch, index],
                device_id=(target, core), device_id_type=MESH,
            ).start()

        everyone(send)

    def arrive(batch):
        f, first, rows = BATCHES[batch]
        for step in range(16):
            source = (row + 4 - FAR_LINES[step // 4]) % 4 * 4 + (column + 4 - FAR_LINES[step % 4]) % 4
            part = data.at[f, :, source, pl.ds(first // 2, rows // 2)]
            pltpu.make_async_copy(part, part, in_sems.at[batch, step]).wait()

    unit = one_hot(iota((LANES, LANES), 0) == iota((LANES, LANES), 1))

    def turn(f):
        return lax.dot_general(
            unit, data.at[f].reshape(HALF, LANES)[...], NT, preferred_element_type=F32
        ).astype(BF16)

    def project(turned, slot):
        return jnp.dot(turned[32 * slot : 32 * slot + 32], table[slot], preferred_element_type=F32)

    lax.fori_loop(0, 4, prepare, 0)
    pl.semaphore_wait(barrier, 23)
    greet_plane(meet)
    lax.fori_loop(4, 8, prepare, 0)
    transform(0)
    publish(0)
    pl.semaphore_wait(meet, 15)
    send_all(0)
    transform(1)
    publish(1)
    send_all(1)
    for slot in range(4):
        table_copy(slot).start()

    transform(2)
    publish(2)
    send_all(2)
    for slot in range(4):
        table_share(slot).start()

    fold_lane = iota((HALF, 2 * LANES), 1)
    fold_turn = fold_lane % 64 // 8
    fold_mask[...] = one_hot(
        (iota((HALF, 2 * LANES), 0) % 10 == fold_lane % LANES // 64 * 5 + fold_turn) & (fold_turn < 5)
    )
    fold_rows[...] = one_hot(iota((LANES, HALF), 1) // 10 == iota((LANES, HALF), 0))
    spread_row = iota((16, 2 * LANES), 0)
    spread_lane = iota((16, 2 * LANES), 1)
    spread = one_hot((spread_row % 2 == spread_lane // LANES) & (spread_row // 2 == spread_lane % 8))

    shape = (16, HALF)
    col = iota(shape, 1)
    even_col = col % 2 == 0
    is_real = iota(shape, 0) % 2 == 0

    def times_unit(values):
        return jnp.where(is_real, -pltpu.roll(values, 15, 0), pltpu.roll(values, 1, 0))

    def neighbours(slot, values):
        wave, last = waves[slot]
        flow = jnp.where(even_col, values[:16], values[16:])
        flow = jnp.where(wave + col <= last, flow, 0.0)
        before = jnp.where(col == 0, 0.0, pltpu.roll(flow, 1, 1))
        after = jnp.where(col == HALF - 1, 0.0, pltpu.roll(flow, HALF - 1, 1))
        return before, flow, after

    waves = []
    for slot in range(4):
        hits = ((owner_ref[...] == me) & (rank == float(slot))).astype(F32)
        used = jnp.sum(hits)
        wave = jnp.where(used > 0, jnp.sum(hits * window), float(HALF)).astype(I32)
        waves.append((wave, jnp.where(used > 0, 2 * HALF - 1, -1)))
        degree_row = wave + iota((8, HALF), 1)
        degree = degree_row.astype(F32)
        next_row = degree_row + 1
        squared = wave * wave
        eps_here = jnp.sqrt((degree_row * degree_row - squared).astype(F32) / (4.0 * degree * degree - 1.0))
        eps_next = jnp.sqrt(
            (next_row * next_row - squared).astype(F32) / (4.0 * (degree + 1.0) * (degree + 1.0) - 1.0)
        )
        factor = lax.rsqrt(degree * (degree + 1.0))
        terms[slot, 0] = (degree + 1.0) * eps_here * factor
        terms[slot, 1] = degree * eps_next * factor
        terms[slot, 2] = wave.astype(F32) * factor
    summed[...] = jnp.zeros_like(summed)

    arrive(0)
    arrive(1)
    turned = turn(0)
    for slot in range(4):
        table_ready(slot)
        before, flow, after = neighbours(slot, project(turned, slot))
        partial[slot, 0] = terms[slot, 0, :1] * before - terms[slot, 1, :1] * after
        partial[slot, 1] = terms[slot, 2, :1] * times_unit(flow)

    own_levels = pl.ds(core * 8, 8)

    def hand_over(slot):
        return pltpu.make_async_remote_copy(
            src_ref=coeffs_out.at[slot], dst_ref=coeffs.at[slot, :, own_levels],
            send_sem=coeffs_send.at[slot], recv_sem=coeffs_recv.at[slot],
            device_id=(me, other), device_id_type=MESH,
        )

    arrive(2)
    turned = turn(1)
    for slot in range(4):
        wave, last = waves[slot]
        live = wave + col <= last
        before, flow, after = neighbours(slot, project(turned, slot))
        vorticity = partial[slot, 0] + terms[slot, 2, :1] * times_unit(flow)
        divergence = partial[slot, 1] - terms[slot, 0, :1] * before + terms[slot, 1, :1] * after
        vorticity = jnp.where(live, vorticity, 0.0)
        divergence = jnp.where(live, divergence, 0.0)
        for q, values in enumerate((vorticity, divergence)):
            lower, upper = values[:, :COLS], values[:, COLS:]
            coeffs[slot, q, own_levels] = jnp.where(core == 0, lower, upper).reshape(8, 2, COLS)
            coeffs_out[slot, q] = jnp.where(core == 0, upper, lower).reshape(8, 2, COLS)
        hand_over(slot).start()
        vorticity = vorticity * vorticity
        divergence = divergence * divergence
        energy = jnp.where(
            is_real,
            vorticity + pltpu.roll(vorticity, 15, 0),
            divergence + pltpu.roll(divergence, 1, 0),
        )
        summed[...] += pltpu.roll(energy, wave - HALF, 1)

    upright = jnp.transpose(summed[...], (1, 0)).astype(BF16)
    placed = jnp.dot(upright, spread, preferred_element_type=F32).astype(BF16) * fold_mask[...]
    messages = jnp.dot(fold_rows[...], placed, preferred_element_type=F32)
    for half in range(2):
        fold_out[:, half, :] = messages[:, LANES * half : LANES * half + LANES]
    fold_in[me] = fold_out[me]

    def send_fold(target, index):
        pltpu.make_async_remote_copy(
            src_ref=fold_out.at[target], dst_ref=fold_in.at[me],
            send_sem=fold_sems.at[0], recv_sem=fold_sems.at[1],
            device_id=(target, core), device_id_type=MESH,
        ).start()

    everyone(send_fold)
    arrived = fold_in.at[pl.ds(0, 127)]
    pltpu.make_async_copy(arrived, arrived, fold_sems.at[1]).wait()
    lines = fold_in.reshape(2 * LANES, LANES)
    folded = lines[0:8, :]
    for index in range(1, 32):
        folded = folded + lines[8 * index : 8 * index + 8, :]
    final[core] = folded[0:2] + folded[2:4] + folded[4:6] + folded[6:8]
    swap = pltpu.make_async_remote_copy(
        src_ref=final.at[core], dst_ref=final.at[core],
        send_sem=final_sems.at[0], recv_sem=final_sems.at[1],
        device_id=(me, other), device_id_type=MESH,
    )
    swap.start()
    for batch in range(3):
        sent = outgoing[batch].at[pl.ds(0, 127)]
        pltpu.make_async_copy(sent, sent, out_sems.at[batch]).wait()
    for slot in range(4):
        table_share(slot).wait_send()
        hand_over(slot).wait_send()
        half = coeffs.at[slot, :, pl.ds(other * 8, 8)]
        pltpu.make_async_copy(half, half, coeffs_recv.at[slot]).wait()
    sent = fold_out.at[pl.ds(0, 127)]
    pltpu.make_async_copy(sent, sent, fold_sems.at[0]).wait()
    swap.wait()
    halves = []
    for half in range(2):
        values = final[half] * (1.0 / ENTRIES)
        halves.append(jnp.where(core == 1, pltpu.roll(values, 64, 1), values))
    for index in range(5):
        spectra_ref[index] = stack([values[:, 8 * index : 8 * index + 8] for values in halves], 1)


def tiles(wind):
    split = wind.transpose(0, 2, 1, 3).reshape(8, ROWS, 2, COARSE, LANES)
    return split.transpose(0, 1, 3, 2, 4)


def local(wind_u, wind_v, window_m, owner, legendre):
    vmem = pl.BlockSpec(memory_space=pltpu.VMEM)
    hbm = pl.BlockSpec(memory_space=pl.ANY)
    dma = pltpu.SemaphoreType.DMA
    coeffs, spectra = pl.pallas_call(
        kernel,
        out_shape=(pltpu.VMEM((4, 2, 16, 2, COLS), F32), pltpu.VMEM((5, 2, 16), F32)),
        in_specs=[hbm, hbm, vmem, vmem, hbm],
        out_specs=(vmem, vmem),
        scratch_shapes=[
            *[pltpu.VMEM((COARSE, 8, rows, 2, LANES), BF16) for _, _, rows in BATCHES],
            pltpu.VMEM((COARSE, ENTRIES), F32),
            pltpu.VMEM((COARSE, ENTRIES), F32),
            pltpu.VMEM((LANES, ENTRIES), F32),
            pltpu.VMEM((LANES, ENTRIES), F32),
            pltpu.VMEM((2 * NLON, 2 * ENTRIES), BF16),
            pltpu.VMEM((160, 2 * ENTRIES), F32),
            pltpu.VMEM((4, 192, LANES), F32),
            *[pltpu.VMEM((128, rows // 2, 2, LANES), BF16) for _, _, rows in BATCHES],
            pltpu.VMEM((2, 8, 16, 5, 2, LANES), BF16),
            pltpu.VMEM((4, HALF, HALF), BF16),
            pltpu.VMEM((4, 3, 8, HALF), F32),
            pltpu.VMEM((4, 2, 16, HALF), F32),
            pltpu.VMEM((16, HALF), F32),
            pltpu.VMEM((4, 2, 8, 2, COLS), F32),
            pltpu.VMEM((HALF, 2 * LANES), BF16),
            pltpu.VMEM((LANES, HALF), BF16),
            pltpu.VMEM((LANES, 2, LANES), F32),
            pltpu.VMEM((LANES, 2, LANES), F32),
            pltpu.VMEM((2, 2, LANES), F32),
            dma((3, STEPS)), dma((4,)), dma((4,)), dma((4,)), pltpu.SemaphoreType.REGULAR,
            dma((3,)), dma((3, 16)), dma((4,)), dma((4,)), dma((2,)), dma((2,)),
        ],
        compiler_params=pltpu.CompilerParams(
            collective_id=0, has_side_effects=True, vmem_limit_bytes=VMEM_BYTES
        ),
    )(tiles(wind_u), tiles(wind_v), window_m[None, :], owner[None, :], legendre)
    return (coeffs, spectra.transpose(1, 2, 0))


def solution(mesh):
    placed = (
        P("deg", None, "wave", None),
        P("deg", None, "wave", None),
        P(),
        P(),
        P("wave", None, "deg"),
    )
    return jax.shard_map(
        local,
        mesh=mesh,
        in_specs=placed,
        out_specs=(P("wave", None, None, None, "deg"), P(None, None, ("wave", "deg"))),
        check_vma=False,
    )
```

```python
import math

import jax
import jax.numpy as jnp
from jax import lax
from jax.experimental import pallas as pl
from jax.experimental.pallas import tpu as pltpu
from jax.sharding import PartitionSpec as P

MESH = pl.DeviceIdType.MESH
BF16 = jnp.bfloat16
F32 = jnp.float32
I32 = jnp.int32
VMEM_BYTES = 56 * 1024 * 1024

NLON = 5120
LANES = 128
COARSE = NLON // LANES
ENTRIES = 256
ROWS = 10
HALF = 1280
COLS = 640
CHUNK = 40
STEPS = COARSE // CHUNK

NT = (((1,), (1,)), ((), ()))
FAR_PLANES = (4, 3, 5, 2, 6, 1, 7, 0)
FAR_LINES = (2, 1, 3, 0)


def iota(shape, axis):
    return lax.broadcasted_iota(I32, shape, axis)


def one_hot(hits):
    return hits.astype(F32).astype(BF16)


def row_order():
    wanted = iota((320, 320), 0)
    source = wanted % 2 * 160 + wanted // 16 % 2 * 80 + wanted // 2 % 8 * 10 + wanted // 32
    return one_hot(source == iota((320, 320), 1))


def group_order():
    source = iota((160, 160), 1)
    return one_hot(source % 16 * ROWS + source // 16 == iota((160, 160), 0))


def unit_waves(count, window, period):
    phase = iota((count, ENTRIES), 0).astype(F32) * window
    phase = phase - period * jnp.round(phase * (1.0 / period))
    angle = phase * (2.0 * math.pi / period)
    return jnp.cos(angle), jnp.sin(angle)


def stack(pieces, axis):
    return jnp.concatenate(pieces, axis=axis)


def kernel(
    wind_u, wind_v, window_ref, owner_ref, table_hbm, coeffs, spectra_ref,
    winds, coarse_cos, coarse_sin, fine_cos, fine_sin, waves_table, total, split,
    outgoing, data, table, terms, partial, summed, coeffs_out,
    fold_mask, fold_rows, fold_out, fold_in, final,
    wind_sems, table_sems, share_send, share_recv, meet,
    out_sems, in_sems, coeffs_send, coeffs_recv, fold_sems, final_sems,
):
    me = lax.axis_index("wave")
    core = lax.axis_index("deg")
    other = 1 - core
    plane = me // 16
    inside = me % 16
    row = inside // 4
    column = inside % 4

    planes = [(plane + away) % 8 * 16 for away in FAR_PLANES]

    def group_base(index):
        turn_x = index // 4
        turn_y = index % 4
        away_x = 2 + (turn_x + 1) // 2 * (1 - 2 * (turn_x % 2))
        away_y = 2 + (turn_y + 1) // 2 * (1 - 2 * (turn_y % 2))
        return (row + away_x) % 4 * 4 + (column + away_y) % 4

    def everyone(action):
        def group(index, carry):
            base = group_base(index)
            for start in planes:
                action(start + base, index)
            return carry

        lax.fori_loop(0, 15, group, 0)
        for start in planes[:7]:
            action(start + inside, 15)

    def wind_copy(f, tile):
        ref = (wind_u, wind_v)[f]
        return pltpu.make_async_copy(ref.at[:, tile], winds.at[f, tile], wind_sems.at[f, tile // CHUNK])

    for tile in range(COARSE):
        wind_copy(0, tile).start()
    def greet_plane(sem):
        def greet(step, carry):
            there = plane * 16 + (inside + step) % 16
            pl.semaphore_signal(sem, inc=1, device_id=(there, core), device_id_type=MESH)
            return carry

        lax.fori_loop(1, 16, greet, 0)

    def greet_line(step, carry):
        there = (plane + step) % 8 * 16 + inside
        pl.semaphore_signal(barrier, inc=1, device_id=(there, core), device_id_type=MESH)
        return carry

    barrier = pltpu.get_barrier_semaphore()
    pl.semaphore_signal(barrier, inc=1, device_id=(me, other), device_id_type=MESH)
    lax.fori_loop(1, 8, greet_line, 0)
    greet_plane(barrier)

    own_half = pl.ds(pl.multiple_of(core * COLS, LANES), COLS)

    def table_copy(slot):
        return pltpu.make_async_copy(table_hbm.at[slot], table.at[slot, :, own_half], table_sems.at[slot])

    def table_share(slot):
        return pltpu.make_async_remote_copy(
            src_ref=table_hbm.at[slot], dst_ref=table.at[slot, :, own_half],
            send_sem=share_send.at[slot], recv_sem=share_recv.at[slot],
            device_id=(me, other), device_id_type=MESH,
        )

    def table_ready(slot):
        table_copy(slot).wait()
        half = table.at[slot, :, pl.ds(pl.multiple_of(other * COLS, LANES), COLS)]
        pltpu.make_async_copy(half, half, share_recv.at[slot]).wait()

    window = window_ref[...].astype(F32)
    owner = owner_ref[...].astype(F32)
    owner_rows = jnp.broadcast_to(owner, (ENTRIES, ENTRIES))
    same = (jnp.transpose(owner_rows, (1, 0)) == owner_rows) & (
        iota((ENTRIES, ENTRIES), 0) < iota((ENTRIES, ENTRIES), 1)
    )
    rank = jnp.sum(same.astype(F32), axis=0, keepdims=True)
    placing = one_hot(owner_ref[...] == iota((128, ENTRIES), 0))
    rank_masks = [one_hot(rank == float(slot)) for slot in range(4)]

    cos_part, sin_part = unit_waves(COARSE, window, float(COARSE))
    coarse_cos[...] = cos_part
    coarse_sin[...] = sin_part
    cos_part, sin_part = unit_waves(LANES, window, float(NLON))
    fine_cos[...] = cos_part * (1.0 / NLON)
    fine_sin[...] = sin_part * (1.0 / NLON)

    def wind_chunk(f, chunk):
        part = winds.at[f, pl.ds(chunk * CHUNK, CHUNK)]
        pltpu.make_async_copy(part, part, wind_sems.at[f, chunk]).wait()
        return stack(
            [winds.at[f, chunk * CHUNK + inner].reshape(160, LANES)[...] for inner in range(CHUNK)], 1
        )

    def prepare(step, carry):
        cos_b = fine_cos[...]
        sin_b = fine_sin[...]
        for inner in range(5):
            tile = step * 5 + inner
            wind_copy(1, tile).start()
            cos_a = coarse_cos[pl.ds(tile, 1), :]
            sin_a = coarse_sin[pl.ds(tile, 1), :]
            values = stack([cos_a * cos_b - sin_a * sin_b, -(sin_a * cos_b + cos_a * sin_b)], 1)
            high = values.astype(BF16)
            first = (tile // CHUNK * CHUNK + tile) * LANES
            waves_table[pl.ds(pl.multiple_of(first, LANES), LANES), :] = high
            second = first + CHUNK * LANES
            low = (values - high.astype(F32)).astype(BF16)
            waves_table[pl.ds(pl.multiple_of(second, LANES), LANES), :] = low
        return carry

    def transform(f):
        def step(chunk, carry):
            part = wind_chunk(f, chunk)
            depth = 2 * CHUNK * LANES
            here = pl.ds(pl.multiple_of(chunk * depth, depth), depth)
            total[...] += jnp.dot(
                stack([part, part], 1), waves_table[here, :], preferred_element_type=F32
            )
            return carry

        total[...] = jnp.zeros_like(total)
        lax.fori_loop(0, STEPS, step, 0)

    def publish(f):
        for tile in range(4):
            split[tile, :160] = total[:, LANES * tile : LANES * tile + LANES]
        north = stack([split[tile, pl.ds(0, 80, stride=2), :] for tile in range(4)], 1)
        south = stack([split[tile, pl.ds(1, 80, stride=2), :] for tile in range(4)], 1)
        even = (north + south).astype(BF16)
        odd = (north - south).astype(BF16)
        paired = stack([even[:, :ENTRIES], odd[:, :ENTRIES], even[:, ENTRIES:], odd[:, ENTRIES:]], 0)
        ordered = jnp.dot(row_order(), paired, preferred_element_type=F32).astype(BF16)
        blocks = stack(
            [
                ordered[32 * line : 32 * line + 32] * rank_masks[slot]
                for line in range(ROWS)
                for slot in range(4)
            ],
            0,
        )
        placed = lax.dot_general(placing, blocks, NT, preferred_element_type=F32).astype(BF16)
        stacked = stack(
            [
                stack(
                    [placed[16 * g : 16 * g + 16, LANES * line : LANES * line + LANES] for g in range(8)], 1
                )
                for line in range(ROWS)
            ],
            0,
        )
        result = jnp.dot(group_order(), stacked, preferred_element_type=F32).astype(BF16)
        flat = outgoing.at[f].reshape(HALF, LANES)
        for g in range(8):
            flat[160 * g : 160 * g + 160, :] = result[:, LANES * g : LANES * g + LANES]

    def own_copy(f):
        return pltpu.make_async_copy(
            outgoing.at[f, me], data.at[f, plane, inside], in_sems.at[f, 15]
        )

    def send_all(f):
        own_copy(f).start()

        def send(target, index):
            pltpu.make_async_remote_copy(
                src_ref=outgoing.at[f, target], dst_ref=data.at[f, plane, inside],
                send_sem=out_sems.at[f], recv_sem=in_sems.at[f, index],
                device_id=(target, core), device_id_type=MESH,
            ).start()

        everyone(send)

    def arrive(f):
        for step in range(16):
            source = (row + 4 - FAR_LINES[step // 4]) % 4 * 4 + (column + 4 - FAR_LINES[step % 4]) % 4
            part = data.at[f, :, source]
            pltpu.make_async_copy(part, part, in_sems.at[f, step]).wait()

    unit = one_hot(iota((LANES, LANES), 0) == iota((LANES, LANES), 1))

    def turn(f):
        return lax.dot_general(
            unit, data.at[f].reshape(HALF, LANES)[...], NT, preferred_element_type=F32
        ).astype(BF16)

    def project(turned, slot):
        return jnp.dot(turned[32 * slot : 32 * slot + 32], table[slot], preferred_element_type=F32)

    lax.fori_loop(0, 8, prepare, 0)
    pl.semaphore_wait(barrier, 23)
    greet_plane(meet)
    transform(0)
    publish(0)
    pl.semaphore_wait(meet, 15)
    send_all(0)
    for slot in range(4):
        table_copy(slot).start()

    transform(1)
    publish(1)
    send_all(1)
    for slot in range(4):
        table_share(slot).start()

    fold_lane = iota((HALF, 2 * LANES), 1)
    fold_turn = fold_lane % 64 // 8
    fold_mask[...] = one_hot(
        (iota((HALF, 2 * LANES), 0) % 10 == fold_lane % LANES // 64 * 5 + fold_turn) & (fold_turn < 5)
    )
    fold_rows[...] = one_hot(iota((LANES, HALF), 1) // 10 == iota((LANES, HALF), 0))
    pair_row = iota((2 * LANES, 2 * LANES), 0)
    interleave = one_hot(pair_row % 2 * LANES + pair_row // 2 == iota((2 * LANES, 2 * LANES), 1))
    spread_row = iota((16, 2 * LANES), 0)
    spread_lane = iota((16, 2 * LANES), 1)
    spread = one_hot((spread_row % 2 == spread_lane // LANES) & (spread_row // 2 == spread_lane % 8))

    shape = (16, HALF)
    col = iota(shape, 1)
    even_col = col % 2 == 0
    is_real = iota(shape, 0) % 2 == 0

    def times_unit(values):
        return jnp.where(is_real, -pltpu.roll(values, 15, 0), pltpu.roll(values, 1, 0))

    def neighbours(slot, values):
        wave, last = waves[slot]
        flow = jnp.where(even_col, values[:16], values[16:])
        flow = jnp.where(wave + col <= last, flow, 0.0)
        before = jnp.where(col == 0, 0.0, pltpu.roll(flow, 1, 1))
        after = jnp.where(col == HALF - 1, 0.0, pltpu.roll(flow, HALF - 1, 1))
        return before, flow, after

    waves = []
    for slot in range(4):
        hits = ((owner_ref[...] == me) & (rank == float(slot))).astype(F32)
        used = jnp.sum(hits)
        wave = jnp.where(used > 0, jnp.sum(hits * window), float(HALF)).astype(I32)
        waves.append((wave, jnp.where(used > 0, 2 * HALF - 1, -1)))
        degree_row = wave + iota((8, HALF), 1)
        degree = degree_row.astype(F32)
        next_row = degree_row + 1
        squared = wave * wave
        eps_here = jnp.sqrt((degree_row * degree_row - squared).astype(F32) / (4.0 * degree * degree - 1.0))
        eps_next = jnp.sqrt(
            (next_row * next_row - squared).astype(F32) / (4.0 * (degree + 1.0) * (degree + 1.0) - 1.0)
        )
        factor = lax.rsqrt(degree * (degree + 1.0))
        terms[slot, 0] = (degree + 1.0) * eps_here * factor
        terms[slot, 1] = degree * eps_next * factor
        terms[slot, 2] = wave.astype(F32) * factor
    summed[...] = jnp.zeros_like(summed)

    arrive(0)
    turned = turn(0)
    for slot in range(4):
        table_ready(slot)
        before, flow, after = neighbours(slot, project(turned, slot))
        partial[slot, 0] = terms[slot, 0, :1] * before - terms[slot, 1, :1] * after
        partial[slot, 1] = terms[slot, 2, :1] * times_unit(flow)

    own_levels = pl.ds(core * 8, 8)

    def hand_over(slot):
        return pltpu.make_async_remote_copy(
            src_ref=coeffs_out.at[slot], dst_ref=coeffs.at[slot, :, own_levels],
            send_sem=coeffs_send.at[slot], recv_sem=coeffs_recv.at[slot],
            device_id=(me, other), device_id_type=MESH,
        )

    arrive(1)
    turned = turn(1)
    for slot in range(4):
        wave, last = waves[slot]
        live = wave + col <= last
        before, flow, after = neighbours(slot, project(turned, slot))
        vorticity = partial[slot, 0] + terms[slot, 2, :1] * times_unit(flow)
        divergence = partial[slot, 1] - terms[slot, 0, :1] * before + terms[slot, 1, :1] * after
        vorticity = jnp.where(live, vorticity, 0.0)
        divergence = jnp.where(live, divergence, 0.0)
        for q, values in enumerate((vorticity, divergence)):
            lower, upper = values[:, :COLS], values[:, COLS:]
            coeffs[slot, q, own_levels] = jnp.where(core == 0, lower, upper).reshape(8, 2, COLS)
            coeffs_out[slot, q] = jnp.where(core == 0, upper, lower).reshape(8, 2, COLS)
        hand_over(slot).start()
        vorticity = vorticity * vorticity
        divergence = divergence * divergence
        energy = jnp.where(
            is_real,
            vorticity + pltpu.roll(vorticity, 15, 0),
            divergence + pltpu.roll(divergence, 1, 0),
        )
        summed[...] += pltpu.roll(energy, wave - HALF, 1)

    upright = jnp.transpose(summed[...], (1, 0)).astype(BF16)
    placed = jnp.dot(upright, spread, preferred_element_type=F32).astype(BF16) * fold_mask[...]
    messages = jnp.dot(fold_rows[...], placed, preferred_element_type=F32)
    messages = messages.astype(BF16)
    messages = stack([messages[:, :LANES], messages[:, LANES:]], 0)
    fold_out.reshape(2 * LANES, LANES)[...] = jnp.dot(
        interleave, messages, preferred_element_type=F32
    ).astype(BF16)
    fold_in[me] = fold_out[me]

    def send_fold(target, index):
        pltpu.make_async_remote_copy(
            src_ref=fold_out.at[target], dst_ref=fold_in.at[me],
            send_sem=fold_sems.at[0], recv_sem=fold_sems.at[1],
            device_id=(target, core), device_id_type=MESH,
        ).start()

    everyone(send_fold)
    arrived = fold_in.at[pl.ds(0, 127)]
    pltpu.make_async_copy(arrived, arrived, fold_sems.at[1]).wait()
    lines = fold_in.reshape(2 * LANES, LANES)[...].astype(F32)
    folded = lines[0:8]
    for index in range(1, 32):
        folded = folded + lines[8 * index : 8 * index + 8]
    final[core] = folded[0:2] + folded[2:4] + folded[4:6] + folded[6:8]
    swap = pltpu.make_async_remote_copy(
        src_ref=final.at[core], dst_ref=final.at[core],
        send_sem=final_sems.at[0], recv_sem=final_sems.at[1],
        device_id=(me, other), device_id_type=MESH,
    )
    swap.start()
    for f in range(2):
        sent = outgoing.at[f, pl.ds(0, 127)]
        pltpu.make_async_copy(sent, sent, out_sems.at[f]).wait()
    for slot in range(4):
        table_share(slot).wait_send()
        hand_over(slot).wait_send()
        half = coeffs.at[slot, :, pl.ds(other * 8, 8)]
        pltpu.make_async_copy(half, half, coeffs_recv.at[slot]).wait()
    sent = fold_out.at[pl.ds(0, 127)]
    pltpu.make_async_copy(sent, sent, fold_sems.at[0]).wait()
    swap.wait()
    halves = []
    for half in range(2):
        values = final[half] * (1.0 / ENTRIES)
        halves.append(jnp.where(core == 1, pltpu.roll(values, 64, 1), values))
    for index in range(5):
        spectra_ref[index] = stack([values[:, 8 * index : 8 * index + 8] for values in halves], 1)


def tiles(wind):
    split = wind.transpose(0, 2, 1, 3).reshape(8, ROWS, 2, COARSE, LANES)
    return split.transpose(0, 1, 3, 2, 4).reshape(80, COARSE, 2, LANES)


def local(wind_u, wind_v, window_m, owner, legendre):
    vmem = pl.BlockSpec(memory_space=pltpu.VMEM)
    hbm = pl.BlockSpec(memory_space=pl.ANY)
    dma = pltpu.SemaphoreType.DMA
    coeffs, spectra = pl.pallas_call(
        kernel,
        out_shape=(pltpu.VMEM((4, 2, 16, 2, COLS), F32), pltpu.VMEM((5, 2, 16), F32)),
        in_specs=[hbm, hbm, vmem, vmem, hbm],
        out_specs=(vmem, vmem),
        scratch_shapes=[
            pltpu.VMEM((2, COARSE, 80, 2, LANES), BF16),
            pltpu.VMEM((COARSE, ENTRIES), F32),
            pltpu.VMEM((COARSE, ENTRIES), F32),
            pltpu.VMEM((LANES, ENTRIES), F32),
            pltpu.VMEM((LANES, ENTRIES), F32),
            pltpu.VMEM((2 * NLON, 2 * ENTRIES), BF16),
            pltpu.VMEM((160, 2 * ENTRIES), F32),
            pltpu.VMEM((4, 192, LANES), F32),
            pltpu.VMEM((2, 128, 5, 2, LANES), BF16),
            pltpu.VMEM((2, 8, 16, 5, 2, LANES), BF16),
            pltpu.VMEM((4, HALF, HALF), BF16),
            pltpu.VMEM((4, 3, 8, HALF), F32),
            pltpu.VMEM((4, 2, 16, HALF), F32),
            pltpu.VMEM((16, HALF), F32),
            pltpu.VMEM((4, 2, 8, 2, COLS), F32),
            pltpu.VMEM((HALF, 2 * LANES), BF16),
            pltpu.VMEM((LANES, HALF), BF16),
            pltpu.VMEM((LANES, 2, LANES), BF16),
            pltpu.VMEM((LANES, 2, LANES), BF16),
            pltpu.VMEM((2, 2, LANES), F32),
            dma((2, STEPS)), dma((4,)), dma((4,)), dma((4,)), pltpu.SemaphoreType.REGULAR,
            dma((2,)), dma((2, 16)), dma((4,)), dma((4,)), dma((2,)), dma((2,)),
        ],
        compiler_params=pltpu.CompilerParams(
            collective_id=0, has_side_effects=True, vmem_limit_bytes=VMEM_BYTES
        ),
    )(tiles(wind_u), tiles(wind_v), window_m[None, :], owner[None, :], legendre)
    return (coeffs, spectra.transpose(1, 2, 0))


def solution(mesh):
    placed = (
        P("deg", None, "wave", None),
        P("deg", None, "wave", None),
        P(),
        P(),
        P("wave", None, "deg"),
    )
    return jax.shard_map(
        local,
        mesh=mesh,
        in_specs=placed,
        out_specs=(P("wave", None, None, None, "deg"), P(None, None, ("wave", "deg"))),
        check_vma=False,
    )
```
